512 devices in a mesh: rec: 32 (over x_hi, z), lig: 16 (over y, x_lo, core).
Axes of the slice: x: 4 (x_hi: 2, x_lo: 2; x = x_hi * 2 + x_lo), y: 4, z: 16, core: 2. Of those that a mesh axis runs over, the one named last changes fastest.
Arguments:
- receptor: bfloat16 [32, 4, 32, 1024], P('rec', None, 'lig'), may hold values from -6 to 6
- ligand_pool: bfloat16 [16, 32, 2, 4, 32, 1024], P('lig', 'rec'), may hold values from -6 to 6
- channel_weight: float32 [4], replicated, may hold values from -3 to 3
- owners: int32 [16, 2], P('lig'), may hold values from 0 to 31
- rotations: int32 [16, 2, 2], P('lig'), may hold values from 0 to 1, each once within a row
Outputs:
- scores: bfloat16 [32, 16, 2, 2, 32, 1024], P('rec', 'lig')
- best: float32 [32, 16, 2, 2], P('rec', 'lig')
- best_all: float32 [16, 2, 2], P('lig')
The draws below stay inside these ranges and needn't reach their ends.
Inputs may be any that keep to these rules, and one draw needn't show every extreme that they name: `rotations`: each row of the last dimension holds every grid of the set once.
All inputs are finite; a program needn't handle non-finite values.
Results may differ from the reference program's by a relative error of at most 0.0049.
Values may be sent and summed in bfloat16 or wider, within the bound.
A program may use at most 64 MiB of HBM per device.

```python
import jax
import jax.numpy as jnp
from jax import lax

G = 32
CH = 4
ROT = 2
ROUNDS = 2
RECS = 32
LIGS = 16


def draw_owners(key, part):
    key = jax.random.fold_in(key, 11)
    first, second = jax.random.split(key)
    total = LIGS * ROUNDS
    flat = jax.random.randint(first, (total,), 0, RECS)
    where = jax.random.randint(second, (), 0, total)
    flat = flat.at[where].set(RECS - 1)
    flat = flat.at[(where + 1) % total].set(0)
    return flat.reshape(LIGS, ROUNDS).astype(jnp.int32)


def level_of(key, dims, shards, low, top_value):
    def one(axis_at, shards_of):
        draws = jax.random.uniform(jax.random.fold_in(jax.random.fold_in(key, 6), axis_at), (shards_of,), jnp.float32, low / len(shards), top_value / len(shards))
        return jnp.repeat(jnp.exp(draws), dims[axis_at] // shards_of).reshape((-1,) + (1,) * (len(dims) - axis_at - 1))

    level = one(*shards[0])
    for cut in shards[1:]:
        level = level * one(*cut)
    return level


def gaussian(rng, extent, deviation, most, shards=(), held_as=jnp.bfloat16):
    drawn = jax.random.normal(rng, extent, jnp.float32) * deviation
    if len(shards) > 0:
        drawn = level_of(rng, extent, shards, -0.22, 0.18) * drawn
    return jnp.clip(drawn, min=-most, max=most).astype(held_as)


def setup_inputs(seed: int = 0) -> dict:
    key_list = jax.random.split(jax.random.key(seed), 6)
    receptor = gaussian(key_list[0], (RECS, CH, G, G * G), 1.0, 6.0, ((0, 32), (2, 16)))
    ligand_pool = gaussian(key_list[1], (LIGS, RECS, ROT, CH, G, G * G), 1.0, 6.0, ((0, 16), (1, 32)))
    channel_weight = gaussian(key_list[2], (CH,), 1.0, 3.0, (), jnp.float32)
    owners = draw_owners(jax.random.fold_in(key_list[5], 71), 0)
    rotations = jax.vmap(lambda own: jax.random.permutation(own, ROT))(jax.random.split(key_list[4], LIGS * ROUNDS)).reshape((LIGS, ROUNDS, ROT)).astype(jnp.int32)
    return {"receptor": receptor, "ligand_pool": ligand_pool, "channel_weight": channel_weight, "owners": owners, "rotations": rotations}


def reference(receptor, ligand_pool, channel_weight, owners, rotations):
    grid = receptor.shape[2]
    norm = 1.0 / jnp.sqrt(jnp.float32(CH * grid ** 3))
    rec_grid = receptor.astype(jnp.float32).reshape(RECS, CH, grid, grid, grid)
    rec_spec = jnp.fft.fftn(rec_grid, axes=(2, 3, 4))
    weighted = jnp.conj(rec_spec) * channel_weight[None, :, None, None, None]
    lig_index = jnp.arange(LIGS)[:, None]
    picked = ligand_pool[lig_index, owners]
    round_index = jnp.arange(ROUNDS)[None, :, None]
    picked = picked[jnp.arange(LIGS)[:, None, None], round_index, rotations]
    lig_grid = picked.astype(jnp.float32).reshape(LIGS, ROUNDS, ROT, CH, grid, grid, grid)
    full_spec = jnp.fft.fftn(lig_grid, axes=(4, 5, 6))
    lig_real = lax.optimization_barrier(jnp.real(full_spec).astype(jnp.bfloat16)).astype(jnp.float32)
    lig_imag = lax.optimization_barrier(jnp.imag(full_spec).astype(jnp.bfloat16)).astype(jnp.float32)
    lig_spec = lax.complex(lig_real, lig_imag)

    def one_receptor(spec):
        product = jnp.einsum('cxyz,lkpcxyz->lkpxyz', spec, lig_spec)
        return jnp.real(jnp.fft.ifftn(product, axes=(3, 4, 5))) * norm
    score_map = lax.map(one_receptor, weighted)
    flat = score_map.reshape(RECS, LIGS, ROUNDS, ROT, grid ** 3)
    best = lax.optimization_barrier(jnp.max(flat, axis=-1))
    best_all = lax.optimization_barrier(jnp.max(best, axis=0))
    scores = score_map.reshape(RECS, LIGS, ROUNDS, ROT, grid, grid * grid).astype(jnp.bfloat16)
    return (scores, best, best_all)
```

```python
import functools

import jax
import jax.numpy as jnp
import ml_dtypes
import numpy as np
from jax import lax
from jax.experimental import pallas as pl
from jax.experimental.pallas import tpu as pltpu
from jax.sharding import PartitionSpec as P

MESH = pl.DeviceIdType.MESH
G = 32
CELLS = G * G
HALF = G // 2 + 1
LANES = 128
BLOCKS = -(-G * HALF // LANES)
FREQS = BLOCKS * LANES
BF16 = jnp.bfloat16
F32 = jnp.float32


def split_table(table):
    high = table.astype(np.float32).astype(ml_dtypes.bfloat16)
    low = (table - high.astype(np.float64)).astype(np.float32).astype(ml_dtypes.bfloat16)
    return np.stack([high, low], 0)


def plane_tables():
    freq = np.arange(FREQS)
    used = freq < G * HALF
    ky, kz = freq // HALF, freq % HALF
    cell = np.arange(CELLS)
    y, z = cell // G, cell % G
    angle = 2.0 * np.pi * ((y[:, None] * ky + z[:, None] * kz) % G) / G
    cosine = np.where(used, np.cos(angle), 0.0).reshape(CELLS, BLOCKS, LANES)
    sine = np.where(used, np.sin(angle), 0.0).reshape(CELLS, BLOCKS, LANES)
    table = np.stack([cosine, -sine], 2)
    forward = table.transpose(1, 0, 2, 3).reshape(BLOCKS, CELLS, 2 * LANES)
    inverse = forward.transpose(0, 2, 1)
    weight = np.where(used, np.where((kz == 0) | (kz == G // 2), 1.0, 2.0), 0.0)
    return split_table(forward), split_table(inverse), weight.astype(np.float32).reshape(1, FREQS)


def line_table(rows_in, rows_out, sign):
    group_in, x = rows_in
    group_out, k = rows_out
    angle = 2.0 * np.pi * ((k[:, None] * x[None, :]) % G) / G
    same = group_out[:, None] == group_in[None, :]
    cosine = np.where(same, np.cos(angle), 0.0)
    sine = np.where(same, np.sin(angle), 0.0) * sign
    return split_table(np.block([[cosine, sine], [-sine, cosine]]))


def line_tables():
    row = np.arange(128)
    plain = (row // G, row % G)
    lig = ((row // 64) * 2 + (row // 16) % 2, ((row // 32) % 2) * 16 + row % 16)
    rec = ((row // 2) % 4, (row // 8) * 2 + row % 2)
    return np.stack(
        [line_table(lig, plain, 1.0), line_table(rec, plain, 1.0), line_table(plain, plain, -1.0)], 0
    )


def dot(a, b):
    return jnp.dot(a, b, preferred_element_type=F32)


def split(value):
    high = value.astype(BF16)
    return high, (value - high.astype(F32)).astype(BF16)


def line_transform(table, high, low):
    return dot(table[0], high) + dot(table[0], low) + dot(table[1], high)


def kernel(
    n,
    scale,
    own_ref,
    rec_ref,
    weight_ref,
    owners_ref,
    rotations_ref,
    forward_hbm,
    inverse_hbm,
    lines_ref,
    fold_ref,
    scores_ref,
    best_ref,
    best_all_ref,
    forward,
    inverse,
    gathered,
    rec_all,
    plus,
    minus,
    across,
    stage,
    rec_stage,
    rec_spec,
    lig_spec,
    product,
    back,
    total,
    score_v,
    tops,
    table_sem,
    out_sem,
    plus_send,
    plus_recv,
    minus_send,
    minus_recv,
    across_send,
    across_recv,
    gplus_send,
    gplus_recv,
    gminus_send,
    gminus_recv,
    rec_send,
    rec_recv,
    top_send,
    top_recv,
):
    rec = lax.axis_index("rec")
    lig = lax.axis_index("lig")
    ligs = rec_all.shape[0]
    recs = 2 * n
    half = n // 2
    side = rec // n
    me = lax.rem(rec, n)
    right = side * n + lax.rem(me + 1, n)
    left = side * n + lax.rem(me + n - 1, n)
    partner = lax.rem(rec + n, recs)

    tables = [
        pltpu.make_async_copy(forward_hbm, forward, table_sem.at[0]),
        pltpu.make_async_copy(inverse_hbm, inverse, table_sem.at[1]),
    ]
    for copy in tables:
        copy.start()

    barrier = pltpu.get_barrier_semaphore()
    for step in range(1, recs):
        pl.semaphore_signal(
            barrier, inc=1, device_id={"rec": lax.rem(rec + step, recs)}, device_id_type=MESH
        )
    for step in range(1, ligs):
        pl.semaphore_signal(
            barrier, inc=1, device_id={"lig": lax.rem(lig + step, ligs)}, device_id_type=MESH
        )
    rec_all[lig] = rec_ref[...].astype(F32)
    pl.semaphore_wait(barrier, recs + ligs - 2)

    sent = []

    def send(src, dst, send_sem, recv_sem, **where):
        copy = pltpu.make_async_remote_copy(
            src_ref=src,
            dst_ref=dst,
            send_sem=send_sem,
            recv_sem=recv_sem,
            device_id=where,
            device_id_type=MESH,
        )
        copy.start()
        sent.append(copy)
        return copy

    owner = [owners_ref[0, k] for k in range(2)]
    owner_z = [lax.rem(owner[k], n) for k in range(2)]
    mine = [owner_z[k] == me for k in range(2)]

    far = lax.rem(me + half, n)
    copies_p = [[None, None] for _ in range(half)]
    copies_m = [[None, None] for _ in range(half - 1)]
    copies_p[0][0] = send(own_ref.at[far], plus.at[0, 0], plus_send.at[0, 0], plus_recv.at[0, 0], rec=right)
    near = lax.rem(me + n - (half - 1), n)
    copies_m[0][0] = send(own_ref.at[near], minus.at[0, 0], minus_send.at[0, 0], minus_recv.at[0, 0], rec=left)

    gather = []
    for step in range(1, ligs):
        gather.append(
            send(
                rec_all.at[lig],
                rec_all.at[lig],
                rec_send.at[step],
                rec_recv.at[step],
                lig=lax.rem(lig + step, ligs),
            )
        )

    for t in range(1, half):
        for k in range(2):
            slots = [(copies_p, plus, plus_send, plus_recv, lax.rem(me + half - t, n), right)]
            if t < half - 1:
                slots.append(
                    (copies_m, minus, minus_send, minus_recv, lax.rem(me + n - (half - 1) + t, n), left)
                )
            for copies, slot, send_sem, recv_sem, shard, to in slots:
                if t == 1:
                    if k == 0:
                        copies[0][0].wait_recv()
                        seen = slot[0, 0]
                        slot[0, 1] = jnp.where(mine[1], own_ref[shard], seen)
                        slot[0, 0] = jnp.where(mine[0], own_ref[shard], seen)
                else:
                    copies[t - 1][k].wait_recv()
                    slot[t - 1, k] = jnp.where(mine[k], own_ref[shard], slot[t - 1, k])
                copies[t][k] = send(
                    slot.at[t - 1, k], slot.at[t, k], send_sem.at[t, k], recv_sem.at[t, k], rec=to
                )

    crossed = []
    for k in range(2):
        copies_p[half - 1][k].wait_recv()
        copies_m[half - 2][k].wait_recv()
        away = lax.rem(owner_z[k] - me + n, n)
        value = jnp.where(
            away == 0, own_ref[me], jnp.where(away < half, minus[half - 2, k], plus[half - 1, k])
        )
        across[0, k] = value
        crossed.append(
            send(across.at[0, k], across.at[1, k], across_send.at[k], across_recv.at[k], rec=partner)
        )
    gather_p = [[None, None] for _ in range(half)]
    gather_m = [[None, None] for _ in range(half - 1)]
    for k in range(2):
        crossed[k].wait_recv()
        gathered[me, k] = jnp.where(owner[k] // n == side, across[0, k], across[1, k])
        for t in range(1):
            gather_p[t][k] = send(
                gathered.at[me, k], gathered.at[me, k], gplus_send.at[t, k], gplus_recv.at[t, k], rec=right
            )
            gather_m[t][k] = send(
                gathered.at[me, k], gathered.at[me, k], gminus_send.at[t, k], gminus_recv.at[t, k], rec=left
            )
    for t in range(1, half):
        for k in range(2):
            shard = lax.rem(me + n - t, n)
            gather_p[t - 1][k].wait_recv()
            gather_p[t][k] = send(
                gathered.at[shard, k], gathered.at[shard, k], gplus_send.at[t, k], gplus_recv.at[t, k], rec=right
            )
            gather_m[t - 1][k].wait_recv()
            if t < half - 1:
                shard = lax.rem(me + t, n)
                gather_m[t][k] = send(
                    gathered.at[shard, k], gathered.at[shard, k], gminus_send.at[t, k], gminus_recv.at[t, k], rec=left
                )

    for copy in gather:
        copy.wait_recv()
    for copy in tables:
        copy.wait()
    rows = rec_all[...].reshape(128, CELLS).astype(BF16)
    for block in range(BLOCKS):
        lanes = pl.ds(block * LANES, LANES)
        value = dot(rows, forward[0, block]) + dot(rows, forward[1, block])
        for part in range(2):
            high, low = split(value[:, part * LANES : (part + 1) * LANES])
            rec_stage[0, part * 128 : (part + 1) * 128, lanes] = high
            rec_stage[1, part * 128 : (part + 1) * 128, lanes] = low
    rec_spec[...] = line_transform(lines_ref.at[1], rec_stage[0], rec_stage[1]) * fold_ref[...]

    for k in range(2):
        gather_p[half - 1][k].wait_recv()

    @pl.loop(0, 4)
    def _(group):
        data = gathered[pl.ds(group * 4, 4)].reshape(128, CELLS)
        for block in range(BLOCKS):
            lanes = pl.ds(block * LANES, LANES)
            value = dot(data, forward[0, block]) + dot(data, forward[1, block])
            for part in range(2):
                high, low = split(value[:, part * LANES : (part + 1) * LANES])
                stage[0, part * 128 : (part + 1) * 128, lanes] = high
                stage[1, part * 128 : (part + 1) * 128, lanes] = low
        lig_spec[group] = line_transform(lines_ref.at[0], stage[0], stage[1]).astype(BF16).astype(F32)

    for k in range(2):
        for grid in range(2):
            real = imag = None
            for c in range(4):
                weight = weight_ref[c]
                group, row = grid * 2 + c // 2, (c % 2) * 64 + k * 32
                lr = lig_spec[group, row : row + 32]
                li = lig_spec[group, 128 + row : 128 + row + 32]
                rr = rec_spec[c * 32 : c * 32 + 32] * weight
                ri = rec_spec[128 + c * 32 : 128 + c * 32 + 32] * weight
                pr = rr * lr + ri * li
                pi = rr * li - ri * lr
                real = pr if real is None else real + pr
                imag = pi if imag is None else imag + pi
            at = (k * 2 + grid) * 32
            product[at : at + 32] = real
            product[128 + at : 128 + at + 32] = imag

    high, low = split(product[...])
    back[...] = line_transform(lines_ref.at[2], high, low)
    for block in range(BLOCKS):
        lanes = slice(block * LANES, (block + 1) * LANES)
        value = jnp.concatenate([back[:128, lanes], back[128:, lanes]], 1)
        high, low = split(value)
        part = dot(high, inverse[0, block]) + dot(low, inverse[0, block]) + dot(high, inverse[1, block])
        if block == 0:
            total[...] = part
        else:
            total[...] += part

    sub = lax.broadcasted_iota(jnp.int32, (8, LANES), 0)
    top = jnp.zeros((8, LANES), F32)
    for k in range(2):
        first = total[k * 64 : k * 64 + 32] * scale
        second = total[k * 64 + 32 : k * 64 + 64] * scale
        for j in range(2):
            value = jnp.where(rotations_ref[0, k, j] == 0, first, second)
            score_v[k, j] = value.astype(BF16)
            top = jnp.where(sub == k * 2 + j, jnp.max(value), top)
    out = pltpu.make_async_copy(score_v, scores_ref, out_sem)
    out.start()
    tops[rec] = top
    copies = []
    for step in range(1, recs):
        copies.append(
            send(
                tops.at[rec],
                tops.at[rec],
                top_send.at[step],
                top_recv.at[step],
                rec=lax.rem(rec + step, recs),
            )
        )
    best_ref[...] = top
    for copy in copies:
        copy.wait_recv()
    best_all_ref[...] = jnp.max(tops[...], axis=0)
    for copy in sent:
        copy.wait_send()
    out.wait()


def on_device(receptor, ligand_pool, channel_weight, owners, rotations, n, ligs):
    channels = ligand_pool.shape[3]
    scale = 1.0 / (float(G) ** 3 * float(channels * G**3) ** 0.5)
    forward, inverse, fold = plane_tables()
    lines = line_tables()
    own = ligand_pool.reshape(n, 16, CELLS)
    rec = receptor.reshape(8, CELLS)
    half = n // 2
    vmem = pl.BlockSpec(memory_space=pltpu.VMEM)
    smem = pl.BlockSpec(memory_space=pltpu.SMEM)
    hbm = pl.BlockSpec(memory_space=pl.ANY)
    dma = pltpu.SemaphoreType.DMA
    scores, best, best_all = pl.pallas_call(
        functools.partial(kernel, n, scale),
        out_shape=(
            jax.ShapeDtypeStruct((2, 2, G, CELLS), BF16),
            jax.ShapeDtypeStruct((8, LANES), F32),
            jax.ShapeDtypeStruct((8, LANES), F32),
        ),
        in_specs=[vmem, vmem, smem, smem, smem, hbm, hbm, vmem, vmem],
        out_specs=(hbm, vmem, vmem),
        scratch_shapes=[
            pltpu.VMEM(forward.shape, BF16),
            pltpu.VMEM(inverse.shape, BF16),
            pltpu.VMEM((n, 2, 16, CELLS), BF16),
            pltpu.VMEM((ligs, 8, CELLS), F32),
            pltpu.VMEM((half, 2, 16, CELLS), BF16),
            pltpu.VMEM((half - 1, 2, 16, CELLS), BF16),
            pltpu.VMEM((2, 2, 16, CELLS), BF16),
            pltpu.VMEM((2, 256, FREQS), BF16),
            pltpu.VMEM((2, 256, FREQS), BF16),
            pltpu.VMEM((256, FREQS), F32),
            pltpu.VMEM((4, 256, FREQS), F32),
            pltpu.VMEM((256, FREQS), F32),
            pltpu.VMEM((256, FREQS), F32),
            pltpu.VMEM((128, CELLS), F32),
            pltpu.VMEM((2, 2, G, CELLS), BF16),
            pltpu.VMEM((2 * n, 8, LANES), F32),
            dma((2,)),
            dma,
            dma((half, 2)),
            dma((half, 2)),
            dma((half, 2)),
            dma((half, 2)),
            dma((2,)),
            dma((2,)),
            dma((half, 2)),
            dma((half, 2)),
            dma((half, 2)),
            dma((half, 2)),
            dma((ligs,)),
            dma((ligs,)),
            dma((2 * n,)),
            dma((2 * n,)),
        ],
        compiler_params=pltpu.CompilerParams(
            collective_id=0, has_side_effects=True, vmem_limit_bytes=56 * 2**20
        ),
        cost_estimate=pl.CostEstimate(flops=6 * 10**9, bytes_accessed=12 * 2**20, transcendentals=0),
    )(own, rec, channel_weight, owners, rotations, forward, inverse, lines, fold)
    return (
        scores[None, None],
        best[:4, 0].reshape(1, 1, 2, 2),
        best_all[:4, 0].reshape(1, 2, 2),
    )


def solution(mesh):
    in_specs = (
        P("rec", None, "lig", None),
        P("lig", "rec", None, None, None, None),
        P(),
        P("lig", None),
        P("lig", None, None),
    )
    out_specs = (
        P("rec", "lig", None, None, None, None),
        P("rec", "lig", None, None),
        P("lig", None, None),
    )
    body = functools.partial(on_device, n=mesh.shape["rec"] // 2, ligs=mesh.shape["lig"])
    return jax.shard_map(body, mesh=mesh, in_specs=in_specs, out_specs=out_specs, check_vma=False)
```

```python
import functools

import jax
import jax.numpy as jnp
import ml_dtypes
import numpy as np
from jax import lax
from jax.experimental import pallas as pl
from jax.experimental.pallas import tpu as pltpu
from jax.sharding import PartitionSpec as P

MESH = pl.DeviceIdType.MESH
G = 32
CELLS = G * G
HALF = G // 2 + 1
LANES = 128
BLOCKS = -(-G * HALF // LANES)
FREQS = BLOCKS * LANES
BF16 = jnp.bfloat16
F32 = jnp.float32


def split_table(table):
    high = table.astype(np.float32).astype(ml_dtypes.bfloat16)
    low = (table - high.astype(np.float64)).astype(np.float32).astype(ml_dtypes.bfloat16)
    return np.stack([high, low], 0)


def plane_tables():
    freq = np.arange(FREQS)
    used = freq < G * HALF
    ky, kz = freq // HALF, freq % HALF
    cell = np.arange(CELLS)
    y, z = cell // G, cell % G
    angle = 2.0 * np.pi * ((y[:, None] * ky + z[:, None] * kz) % G) / G
    cosine = np.where(used, np.cos(angle), 0.0).reshape(CELLS, BLOCKS, LANES)
    sine = np.where(used, np.sin(angle), 0.0).reshape(CELLS, BLOCKS, LANES)
    table = np.stack([cosine, -sine], 2)
    forward = table.transpose(1, 0, 2, 3).reshape(BLOCKS, CELLS, 2 * LANES)
    inverse = forward.transpose(0, 2, 1)
    weight = np.where(used, np.where((kz == 0) | (kz == G // 2), 1.0, 2.0), 0.0)
    return split_table(forward), split_table(inverse), weight.astype(np.float32).reshape(1, FREQS)


def line_table(rows_in, rows_out, sign):
    group_in, x = rows_in
    group_out, k = rows_out
    angle = 2.0 * np.pi * ((k[:, None] * x[None, :]) % G) / G
    same = group_out[:, None] == group_in[None, :]
    cosine = np.where(same, np.cos(angle), 0.0)
    sine = np.where(same, np.sin(angle), 0.0) * sign
    return split_table(np.block([[cosine, sine], [-sine, cosine]]))


def line_tables():
    row = np.arange(128)
    plain = (row // G, row % G)
    lig = ((row // 64) * 2 + (row // 16) % 2, ((row // 32) % 2) * 16 + row % 16)
    rec = ((row // 2) % 4, (row // 8) * 2 + row % 2)
    return np.stack(
        [line_table(lig, plain, 1.0), line_table(rec, plain, 1.0), line_table(plain, plain, -1.0)], 0
    )


def dot(a, b):
    return jnp.dot(a, b, preferred_element_type=F32)


def split(value):
    high = value.astype(BF16)
    return high, (value - high.astype(F32)).astype(BF16)


def line_transform(table, high, low):
    return dot(table[0], high) + dot(table[0], low) + dot(table[1], high)


def plane_transform(rows, forward, block):
    value = None
    for half in range(2):
        for part in range(2):
            term = dot(rows[half], forward[part, block, half * COLS : (half + 1) * COLS])
            value = term if value is None else value + term
    return value


NEAR = (-2, -1, 1, 2)
FAR = (-5, 5)
WINDOW = (-2, -1, 1, 2, 3)
COLS = CELLS // 2


def kernel(
    n,
    scale,
    rec_ref,
    weight_ref,
    owners_ref,
    rotations_ref,
    own_hbm,
    forward_hbm,
    inverse_hbm,
    lines_hbm,
    fold_hbm,
    scores_ref,
    best_ref,
    best_all_ref,
    own,
    forward,
    inverse,
    lines,
    fold,
    leaves,
    ends,
    partial,
    roots,
    gathered,
    rec_all,
    stage,
    rec_stage,
    rec_spec,
    lig_spec,
    product,
    back,
    total,
    score_v,
    tops,
    table_sem,
    out_sem,
    leaf_send,
    leaf_recv,
    end_send,
    end_recv,
    root_send,
    root_recv,
    first_send,
    first_recv,
    relay_send,
    relay_recv,
    last_send,
    last_recv,
    cross_send,
    cross_recv,
    rec_send,
    rec_recv,
    top_send,
    top_recv,
):
    rec = lax.axis_index("rec")
    lig = lax.axis_index("lig")
    side = rec // n
    me = lax.rem(rec, n)
    partner = lax.rem(rec + n, 2 * n)

    def shift(step):
        return lax.rem(me + n + step, n)

    def at(step):
        return side * n + shift(step)

    def over(step):
        return (1 - side) * n + shift(step)

    quad = lig // 4
    quad_peers = [quad * 4 + lax.rem(lig + step, 4) for step in range(1, 4)]
    line_peers = [lax.rem(lig + 4 * step, 16) for step in range(1, 4)]

    barrier = pltpu.get_barrier_semaphore()
    rec_peers = [at(step) for step in (-5, -3, -2, -1, 1, 2, 3, 5)] + [over(step) for step in (-5, 0, 5)]
    for peer in rec_peers:
        pl.semaphore_signal(barrier, inc=1, device_id={"rec": peer}, device_id_type=MESH)
    for peer in quad_peers + line_peers:
        pl.semaphore_signal(barrier, inc=1, device_id={"lig": peer}, device_id_type=MESH)

    loads = [
        pltpu.make_async_copy(src, dst, table_sem.at[i])
        for i, (src, dst) in enumerate(
            [(own_hbm, own), (forward_hbm, forward), (lines_hbm, lines), (fold_hbm, fold), (inverse_hbm, inverse)]
        )
    ]
    for copy in loads:
        copy.start()

    slab = jnp.concatenate([rec_ref[c].astype(F32) for c in range(4)], 0)
    rec_all[lig] = jnp.concatenate([slab[:, :COLS], slab[:, COLS:]], 0).astype(BF16)
    loads[0].wait()
    pl.semaphore_wait(barrier, len(rec_peers) + 6)

    sent = []

    def send(src, dst, send_sem, recv_sem, **where):
        copy = pltpu.make_async_remote_copy(
            src_ref=src,
            dst_ref=dst,
            send_sem=send_sem,
            recv_sem=recv_sem,
            device_id=where,
            device_id_type=MESH,
        )
        copy.start()
        sent.append(copy)
        return copy

    owner = [owners_ref[0, k] for k in range(2)]
    owner_z = [lax.rem(owner[k], n) for k in range(2)]
    owner_side = [owner[k] // n for k in range(2)]

    leaf = {}
    for j, step in ((1, -5), (2, 5), (0, 0)):
        for i, to in enumerate(NEAR):
            leaf[i, j] = send(
                own.at[shift(to + step)], leaves.at[i, j], leaf_send.at[i, j], leaf_recv.at[i, j], rec=at(to)
            )
    far = shift(n // 2)
    end = [
        send(own.at[far, :, :COLS], ends.at[0], end_send.at[0], end_recv.at[0], rec=at(-3)),
        send(own.at[far, :, COLS:], ends.at[1], end_send.at[1], end_recv.at[1], rec=at(3)),
    ]
    slabs = [
        send(rec_all.at[lig], rec_all.at[lig], rec_send.at[0, i], rec_recv.at[0, i], lig=peer)
        for i, peer in enumerate(quad_peers)
    ]
    for copy in slabs:
        copy.wait_recv()
    block = rec_all.at[pl.ds(quad * 4, 4)]
    slabs = [
        send(block, block, rec_send.at[1, i], rec_recv.at[1, i], lig=peer) for i, peer in enumerate(line_peers)
    ]

    root = {}
    for j, step in ((1, -5), (2, 5), (0, 0)):
        shard = shift(step)
        for i in range(len(NEAR)):
            leaf[i, j].wait_recv()
        if j:
            end[j - 1].wait_recv()
        for k in range(2):
            away = lax.rem(owner_z[k] - me + n, n)
            value = own[shard]
            for i, to in enumerate(NEAR):
                value = jnp.where(away == (n - to) % n, leaves[i, j], value)
            parts = [value[:, :COLS], value[:, COLS:]]
            if j == 1:
                parts[0] = jnp.where(away == 3, ends[0], parts[0])
            if j == 2:
                parts[1] = jnp.where(away == n - 3, ends[1], parts[1])
            for half in range(2):
                partial[j, half, k] = parts[half]
        if j:
            for half in range(2):
                slot = (j - 1) * 2 + side
                root[j, half] = send(
                    partial.at[j, half],
                    roots.at[slot],
                    root_send.at[j - 1, half],
                    root_recv.at[slot],
                    rec=half * n + shard,
                )
        else:
            root[0] = send(partial.at[0, 1 - side], roots.at[4], root_send.at[2, 0], root_recv.at[4], rec=partner)

    for copy in slabs:
        copy.wait_recv()
    loads[1].wait()
    loads[2].wait()
    loads[3].wait()
    grid = rec_all[...].astype(F32)
    rows = [grid[:, half * 8 : half * 8 + 8].reshape(128, COLS).astype(BF16) for half in range(2)]
    for block in range(BLOCKS):
        lanes = pl.ds(block * LANES, LANES)
        value = plane_transform(rows, forward, block)
        for part in range(2):
            high, low = split(value[:, part * LANES : (part + 1) * LANES])
            rec_stage[0, part * 128 : (part + 1) * 128, lanes] = high
            rec_stage[1, part * 128 : (part + 1) * 128, lanes] = low
    rec_spec[...] = line_transform(lines.at[1], rec_stage[0], rec_stage[1]) * fold[...]

    def root_wait(slot):
        pltpu.make_async_copy(roots.at[slot], roots.at[slot], root_recv.at[slot]).wait()

    for slot in range(5):
        root_wait(slot)
    for k in range(2):
        away = lax.rem(owner_z[k] - me + n, n)
        below = jnp.logical_or(away > n // 2, jnp.logical_and(away == n // 2, side == 1))
        inner = jnp.logical_or(away <= 2, away >= n - 2)
        here = owner_side[k] == side
        middle = jnp.where(here, partial[0, side, k], roots[4, k])
        up = jnp.where(owner_side[k] == 0, roots[0, k], roots[1, k])
        down = jnp.where(owner_side[k] == 0, roots[2, k], roots[3, k])
        gathered[me, side, k] = jnp.where(inner, middle, jnp.where(below, down, up))

    cross = []

    def spread(shard, lo=0, hi=2):
        ref = gathered.at[shard, side, lo:hi]
        slot = len(cross)
        cross.append(send(ref, ref, cross_send.at[slot], cross_recv.at[slot], rec=partner))

    mine = gathered.at[me, side]
    first = {}
    for i, to in enumerate(FAR + NEAR):
        first[to] = send(mine, mine, first_send.at[i], first_recv.at[i], rec=at(to))
    spread(me)
    relay = {}
    last = []
    for j, to in enumerate(FAR):
        first[to].wait_recv()
        shard = shift(-to)
        ref = gathered.at[shard, side]
        for i, near in enumerate(NEAR):
            relay[i, j] = send(ref, ref, relay_send.at[i, j], relay_recv.at[i, j], rec=at(near))
        ref = gathered.at[shard, side, j]
        last.append(send(ref, ref, last_send.at[j], last_recv.at[j], rec=at(-3 if to < 0 else 3)))
        spread(shard)
    for to in NEAR:
        first[to].wait_recv()
        spread(shift(-to))
    for j, to in enumerate(FAR):
        for i, near in enumerate(NEAR):
            relay[i, j].wait_recv()
            spread(shift(-near - to))
    for j in range(2):
        last[j].wait_recv()
        spread(far, j, j + 1)
    for copy in cross:
        copy.wait_recv()

    @pl.loop(0, 4)
    def _(group):
        data = [gathered[pl.ds(group * 4, 4), half].reshape(128, COLS) for half in range(2)]
        for block in range(BLOCKS):
            lanes = pl.ds(block * LANES, LANES)
            value = plane_transform(data, forward, block)
            for part in range(2):
                high, low = split(value[:, part * LANES : (part + 1) * LANES])
                stage[0, part * 128 : (part + 1) * 128, lanes] = high
                stage[1, part * 128 : (part + 1) * 128, lanes] = low
        lig_spec[group] = line_transform(lines.at[0], stage[0], stage[1]).astype(BF16).astype(F32)

    for k in range(2):
        for grid in range(2):
            real = imag = None
            for c in range(4):
                weight = weight_ref[c]
                group, row = grid * 2 + c // 2, (c % 2) * 64 + k * 32
                lr = lig_spec[group, row : row + 32]
                li = lig_spec[group, 128 + row : 128 + row + 32]
                rr = rec_spec[c * 32 : c * 32 + 32] * weight
                ri = rec_spec[128 + c * 32 : 128 + c * 32 + 32] * weight
                pr = rr * lr + ri * li
                pi = rr * li - ri * lr
                real = pr if real is None else real + pr
                imag = pi if imag is None else imag + pi
            row = (k * 2 + grid) * 32
            product[row : row + 32] = real
            product[128 + row : 128 + row + 32] = imag

    loads[4].wait()
    high, low = split(product[...])
    back[...] = line_transform(lines.at[2], high, low)
    for block in range(BLOCKS):
        lanes = slice(block * LANES, (block + 1) * LANES)
        value = jnp.concatenate([back[:128, lanes], back[128:, lanes]], 1)
        high, low = split(value)
        part = dot(high, inverse[0, block]) + dot(low, inverse[0, block]) + dot(high, inverse[1, block])
        if block == 0:
            total[...] = part
        else:
            total[...] += part

    sub = lax.broadcasted_iota(jnp.int32, (8, LANES), 0)
    lane = lax.broadcasted_iota(jnp.int32, (8, LANES), 1)
    top = jnp.zeros((8, LANES), F32)
    for k in range(2):
        pair = [total[k * 64 : k * 64 + 32] * scale, total[k * 64 + 32 : k * 64 + 64] * scale]
        for j in range(2):
            value = jnp.where(rotations_ref[0, k, j] == 0, pair[0], pair[1])
            score_v[k, j] = value.astype(BF16)
            top = jnp.where(jnp.logical_and(sub == k, lane == j), jnp.max(value), top)
    out = pltpu.make_async_copy(score_v, scores_ref, out_sem)
    out.start()
    best_ref[0, 0] = top[:2, :2]
    tops[0, 5] = top
    copies = [
        send(tops.at[0, 5], tops.at[0, i], top_send.at[0, i], top_recv.at[0, i], rec=at(-step))
        for i, step in enumerate(WINDOW)
    ]
    for copy in copies:
        copy.wait_recv()
    tops[1, 5] = jnp.max(tops[0], axis=0)
    peers = [at(-5), at(5), over(0), over(-5), over(5)]
    copies = [
        send(tops.at[1, 5], tops.at[1, i], top_send.at[1, i], top_recv.at[1, i], rec=peer)
        for i, peer in enumerate(peers)
    ]
    for copy in copies:
        copy.wait_recv()
    best_all_ref[0] = jnp.max(tops[1], axis=0)[:2, :2]
    for copy in sent:
        copy.wait_send()
    out.wait()


def on_device(receptor, ligand_pool, channel_weight, owners, rotations, n, ligs):
    channels = ligand_pool.shape[3]
    scale = 1.0 / (float(G) ** 3 * float(channels * G**3) ** 0.5)
    forward, inverse, fold = plane_tables()
    lines = line_tables()
    own = ligand_pool.reshape(n, 16, CELLS)
    vmem = pl.BlockSpec(memory_space=pltpu.VMEM)
    smem = pl.BlockSpec(memory_space=pltpu.SMEM)
    hbm = pl.BlockSpec(memory_space=pl.ANY)
    dma = pltpu.SemaphoreType.DMA
    scores, best, best_all = pl.pallas_call(
        functools.partial(kernel, n, scale),
        out_shape=(
            jax.ShapeDtypeStruct((2, 2, G, CELLS), BF16),
            jax.ShapeDtypeStruct((1, 1, 2, 2), F32),
            jax.ShapeDtypeStruct((1, 2, 2), F32),
        ),
        in_specs=[vmem, smem, smem, smem, hbm, hbm, hbm, hbm, hbm],
        out_specs=(hbm, vmem, vmem),
        scratch_shapes=[
            pltpu.VMEM((n, 16, CELLS), BF16),
            pltpu.VMEM(forward.shape, BF16),
            pltpu.VMEM(inverse.shape, BF16),
            pltpu.VMEM(lines.shape, BF16),
            pltpu.VMEM(fold.shape, F32),
            pltpu.VMEM((4, 3, 16, CELLS), BF16),
            pltpu.VMEM((2, 16, COLS), BF16),
            pltpu.VMEM((3, 2, 2, 16, COLS), BF16),
            pltpu.VMEM((5, 2, 16, COLS), BF16),
            pltpu.VMEM((n, 2, 2, 16, COLS), BF16),
            pltpu.VMEM((ligs, 16, COLS), BF16),
            pltpu.VMEM((2, 256, FREQS), BF16),
            pltpu.VMEM((2, 256, FREQS), BF16),
            pltpu.VMEM((256, FREQS), F32),
            pltpu.VMEM((4, 256, FREQS), F32),
            pltpu.VMEM((256, FREQS), F32),
            pltpu.VMEM((256, FREQS), F32),
            pltpu.VMEM((128, CELLS), F32),
            pltpu.VMEM((2, 2, G, CELLS), BF16),
            pltpu.VMEM((2, 6, 8, LANES), F32),
            dma((5,)),
            dma,
            dma((4, 3)),
            dma((4, 3)),
            dma((2,)),
            dma((2,)),
            dma((3, 2)),
            dma((5,)),
            dma((6,)),
            dma((6,)),
            dma((4, 2)),
            dma((4, 2)),
            dma((2,)),
            dma((2,)),
            dma((n + 1,)),
            dma((n + 1,)),
            dma((2, 3)),
            dma((2, 3)),
            dma((2, 5)),
            dma((2, 5)),
        ],
        compiler_params=pltpu.CompilerParams(
            collective_id=0, has_side_effects=True, vmem_limit_bytes=56 * 2**20
        ),
        cost_estimate=pl.CostEstimate(flops=6 * 10**9, bytes_accessed=12 * 2**20, transcendentals=0),
    )(receptor[0], channel_weight, owners, rotations, own, forward, inverse, lines, fold)
    return scores[None, None], best, best_all


def solution(mesh):
    in_specs = (
        P("rec", None, "lig", None),
        P("lig", "rec", None, None, None, None),
        P(),
        P("lig", None),
        P("lig", None, None),
    )
    out_specs = (
        P("rec", "lig", None, None, None, None),
        P("rec", "lig", None, None),
        P("lig", None, None),
    )
    body = functools.partial(on_device, n=mesh.shape["rec"] // 2, ligs=mesh.shape["lig"])
    return jax.shard_map(body, mesh=mesh, in_specs=in_specs, out_specs=out_specs, check_vma=False)
```

```python
import functools

import jax
import jax.numpy as jnp
import ml_dtypes
import numpy as np
from jax import lax
from jax.experimental import pallas as pl
from jax.experimental.pallas import tpu as pltpu
from jax.sharding import PartitionSpec as P

MESH = pl.DeviceIdType.MESH
G = 32
CELLS = G * G
HALF = G // 2 + 1
LANES = 128
BLOCKS = -(-G * HALF // LANES)
FREQS = BLOCKS * LANES
BF16 = jnp.bfloat16
F32 = jnp.float32


def split_table(table):
    high = table.astype(np.float32).astype(ml_dtypes.bfloat16)
    low = (table - high.astype(np.float64)).astype(np.float32).astype(ml_dtypes.bfloat16)
    return np.stack([high, low], 0)


def plane_tables():
    freq = np.arange(FREQS)
    used = freq < G * HALF
    ky, kz = freq // HALF, freq % HALF
    cell = np.arange(CELLS)
    y, z = cell // G, cell % G
    angle = 2.0 * np.pi * ((y[:, None] * ky + z[:, None] * kz) % G) / G
    cosine = np.where(used, np.cos(angle), 0.0).reshape(CELLS, BLOCKS, LANES)
    sine = np.where(used, np.sin(angle), 0.0).reshape(CELLS, BLOCKS, LANES)
    table = np.stack([cosine, -sine], 2)
    forward = table.transpose(1, 0, 2, 3).reshape(BLOCKS, CELLS, 2 * LANES)
    inverse = table.transpose(2, 1, 3, 0).reshape(2 * FREQS, CELLS // 256, 256).transpose(1, 0, 2)
    weight = np.where(used, np.where((kz == 0) | (kz == G // 2), 1.0, 2.0), 0.0)
    return split_table(forward), split_table(inverse), weight.astype(np.float32).reshape(1, FREQS)


def line_table(rows_in, rows_out, sign):
    group_in, x = rows_in
    group_out, k = rows_out
    angle = 2.0 * np.pi * ((k[:, None] * x[None, :]) % G) / G
    same = group_out[:, None] == group_in[None, :]
    cosine = np.where(same, np.cos(angle), 0.0)
    sine = np.where(same, np.sin(angle), 0.0) * sign
    return split_table(np.block([[cosine, sine], [-sine, cosine]]))


def line_tables():
    row = np.arange(128)
    plain = (row // G, row % G)
    rec = ((row // 2) % 4, (row // 8) * 2 + row % 2)
    pair = (plain[0][:64], plain[1][:64])
    forward = np.stack([line_table(plain, plain, 1.0), line_table(rec, plain, 1.0)], 0)
    return forward, line_table(pair, pair, -1.0)


def dot(a, b):
    return jnp.dot(a, b, preferred_element_type=F32)


def split(value):
    high = value.astype(BF16)
    return high, (value - high.astype(F32)).astype(BF16)


def line_transform(table, high, low):
    return dot(table[0], high) + dot(table[0], low) + dot(table[1], high)


def half_plane(data, forward, block, half):
    rows = pl.ds(pl.multiple_of(half * COLS, COLS), COLS)
    return dot(data, forward[0, block, rows]) + dot(data, forward[1, block, rows])


NEAR = (-2, -1, 1, 2)
FAR = (-5, 5)
WINDOW = (-2, -1, 1, 2, 3)
COLS = CELLS // 2


def kernel(
    n,
    scale,
    rec_ref,
    weight_ref,
    owners_ref,
    rotations_ref,
    own_hbm,
    forward_hbm,
    inverse_hbm,
    lines_hbm,
    back_hbm,
    fold_hbm,
    scores_ref,
    tops_ref,
    own,
    forward,
    inverse,
    lines,
    back_lines,
    fold,
    leaves,
    ends,
    partial,
    roots,
    gathered,
    rec_all,
    sums,
    stage,
    rec_stage,
    rec_spec,
    lig_spec,
    product,
    back,
    total,
    score_v,
    tops,
    table_sem,
    out_sem,
    leaf_send,
    leaf_recv,
    end_send,
    end_recv,
    root_send,
    root_recv,
    first_send,
    first_recv,
    relay_send,
    relay_recv,
    last_send,
    last_recv,
    cross_send,
    cross_recv,
    rec_send,
    rec_recv,
    top_send,
    top_recv,
):
    rec = lax.axis_index("rec")
    lig = lax.axis_index("lig")
    side = rec // n
    me = lax.rem(rec, n)
    partner = lax.rem(rec + n, 2 * n)

    def shift(step):
        return lax.rem(me + n + step, n)

    def at(step):
        return side * n + shift(step)

    def over(step):
        return (1 - side) * n + shift(step)

    quad = lig // 4
    quad_peers = [quad * 4 + lax.rem(lig + step, 4) for step in range(1, 4)]
    line_peers = [lax.rem(lig + 4 * step, 16) for step in range(1, 4)]

    barrier = pltpu.get_barrier_semaphore()
    rec_peers = [at(step) for step in (-5, -3, -2, -1, 1, 2, 3, 5)] + [over(step) for step in (-5, 0, 5)]
    for peer in rec_peers:
        pl.semaphore_signal(barrier, inc=1, device_id={"rec": peer}, device_id_type=MESH)
    for peer in quad_peers + line_peers:
        pl.semaphore_signal(barrier, inc=1, device_id={"lig": peer}, device_id_type=MESH)

    loads = [
        pltpu.make_async_copy(src, dst, table_sem.at[i])
        for i, (src, dst) in enumerate(
            [(own_hbm, own), (forward_hbm, forward), (lines_hbm, lines), (fold_hbm, fold), (inverse_hbm, inverse), (back_hbm, back_lines)]
        )
    ]
    for copy in loads:
        copy.start()

    slab = jnp.concatenate([rec_ref[c].astype(F32) for c in range(4)], 0)
    rec_all[lig] = jnp.concatenate([slab[:, :COLS], slab[:, COLS:]], 0).astype(BF16)
    loads[0].wait()
    pl.semaphore_wait(barrier, len(rec_peers) + 6)

    sent = []

    def send(src, dst, send_sem, recv_sem, **where):
        copy = pltpu.make_async_remote_copy(
            src_ref=src,
            dst_ref=dst,
            send_sem=send_sem,
            recv_sem=recv_sem,
            device_id=where,
            device_id_type=MESH,
        )
        copy.start()
        sent.append(copy)
        return copy

    owner = [owners_ref[0, k] for k in range(2)]
    owner_z = [lax.rem(owner[k], n) for k in range(2)]
    owner_side = [owner[k] // n for k in range(2)]

    far = shift(n // 2)
    end = [
        send(own.at[far, :, :COLS], ends.at[0], end_send.at[0], end_recv.at[0], rec=at(-3)),
        send(own.at[far, :, COLS:], ends.at[1], end_send.at[1], end_recv.at[1], rec=at(3)),
    ]
    leaf = {}
    for j, step in ((1, -5), (2, 5), (0, 0)):
        for i, to in enumerate(NEAR):
            leaf[i, j] = send(
                own.at[shift(to + step)], leaves.at[i, j], leaf_send.at[i, j], leaf_recv.at[i, j], rec=at(to)
            )
    slabs = [
        send(rec_all.at[lig], rec_all.at[lig], rec_send.at[0, i], rec_recv.at[0, i], lig=peer)
        for i, peer in enumerate(quad_peers)
    ]
    for copy in slabs:
        copy.wait_recv()
    block = rec_all.at[pl.ds(quad * 4, 4)]
    slabs = [
        send(block, block, rec_send.at[1, i], rec_recv.at[1, i], lig=peer) for i, peer in enumerate(line_peers)
    ]

    root = {}
    for j, step in ((1, -5), (2, 5), (0, 0)):
        shard = shift(step)
        for i in range(len(NEAR)):
            leaf[i, j].wait_recv()
        if j:
            end[j - 1].wait_recv()
        for k in range(2):
            away = lax.rem(owner_z[k] - me + n, n)
            value = own[shard]
            for i, to in enumerate(NEAR):
                value = jnp.where(away == (n - to) % n, leaves[i, j], value)
            parts = [value[:, :COLS], value[:, COLS:]]
            if j == 1:
                parts[0] = jnp.where(away == 3, ends[0], parts[0])
            if j == 2:
                parts[1] = jnp.where(away == n - 3, ends[1], parts[1])
            for half in range(2):
                partial[j, half, k] = parts[half]
            if j:
                for half in range(2):
                    slot = (j - 1) * 2 + side
                    root[j, half, k] = send(
                        partial.at[j, half, k],
                        roots.at[slot, k],
                        root_send.at[j - 1, half, k],
                        root_recv.at[slot, k],
                        rec=half * n + shard,
                    )
            else:
                root[0, k] = send(
                    partial.at[0, 1 - side, k],
                    roots.at[4, k],
                    root_send.at[2, 0, k],
                    root_recv.at[4, k],
                    rec=partner,
                )

    for copy in slabs:
        copy.wait_recv()
    loads[1].wait()
    loads[2].wait()
    loads[3].wait()
    grid = rec_all[...].astype(F32)
    rows = [grid[:, half * 8 : half * 8 + 8].reshape(128, COLS).astype(BF16) for half in range(2)]
    for block in range(BLOCKS):
        lanes = pl.ds(block * LANES, LANES)
        value = half_plane(rows[0], forward, block, 0) + half_plane(rows[1], forward, block, 1)
        for part in range(2):
            high, low = split(value[:, part * LANES : (part + 1) * LANES])
            rec_stage[0, part * 128 : (part + 1) * 128, lanes] = high
            rec_stage[1, part * 128 : (part + 1) * 128, lanes] = low
    rec_spec[...] = line_transform(lines.at[1], rec_stage[0], rec_stage[1]) * fold[...]

    def root_wait(slot, k):
        pltpu.make_async_copy(roots.at[slot, k], roots.at[slot, k], root_recv.at[slot, k]).wait()

    first, relay, last = {}, {}, {}
    cross = [[], []]

    def spread(k, shard):
        ref = gathered.at[k, shard, side]
        slot = len(cross[k])
        cross[k].append(send(ref, ref, cross_send.at[k, slot], cross_recv.at[k, slot], rec=partner))

    def gather_first(k):
        for slot in range(5):
            root_wait(slot, k)
        away = lax.rem(owner_z[k] - me + n, n)
        below = jnp.logical_or(away > n // 2, jnp.logical_and(away == n // 2, side == 1))
        inner = jnp.logical_or(away <= 2, away >= n - 2)
        here = owner_side[k] == side
        middle = jnp.where(here, partial[0, side, k], roots[4, k])
        up = jnp.where(owner_side[k] == 0, roots[0, k], roots[1, k])
        down = jnp.where(owner_side[k] == 0, roots[2, k], roots[3, k])
        gathered[k, me, side] = jnp.where(inner, middle, jnp.where(below, down, up))
        mine = gathered.at[k, me, side]
        for i, to in enumerate(FAR + NEAR):
            first[k, to] = send(mine, mine, first_send.at[i, k], first_recv.at[i, k], rec=at(to))
        spread(k, me)

    def gather_relay(k):
        for j, to in enumerate(FAR):
            first[k, to].wait_recv()
            shard = shift(-to)
            ref = gathered.at[k, shard, side]
            for i, near in enumerate(NEAR):
                relay[i, j, k] = send(ref, ref, relay_send.at[i, j, k], relay_recv.at[i, j, k], rec=at(near))
            if j == k:
                last[k] = send(ref, ref, last_send.at[k], last_recv.at[k], rec=at(-3 if to < 0 else 3))
            spread(k, shard)
        for to in NEAR:
            first[k, to].wait_recv()
            spread(k, shift(-to))

    def gather_cross(k):
        for j, to in enumerate(FAR):
            for i, near in enumerate(NEAR):
                relay[i, j, k].wait_recv()
                spread(k, shift(-near - to))
        last[k].wait_recv()
        spread(k, far)

    for k in range(2):
        gather_first(k)
    for k in range(2):
        gather_relay(k)
    for k in range(2):
        gather_cross(k)

    def half_rows(k, half):
        return gathered[k, :, half].reshape(256, COLS)

    for k in range(2):
        data = half_rows(k, side)
        for block in range(BLOCKS):
            sums[k, block] = half_plane(data, forward, block, side)

    sub = lax.broadcasted_iota(jnp.int32, (8, LANES), 0)
    lane = lax.broadcasted_iota(jnp.int32, (8, LANES), 1)
    top = jnp.zeros((8, LANES), F32)
    for k in range(2):
        for copy in cross[k]:
            copy.wait_recv()

        data = half_rows(k, 1 - side)
        for block in range(BLOCKS):
            lanes = pl.ds(block * LANES, LANES)
            value = sums[k, block] + half_plane(data, forward, block, 1 - side)
            for part in range(2):
                high, low = split(value[:, part * LANES : (part + 1) * LANES])
                for grid in range(2):
                    stage[grid, 0, part * 128 : (part + 1) * 128, lanes] = high[grid * 128 : grid * 128 + 128]
                    stage[grid, 1, part * 128 : (part + 1) * 128, lanes] = low[grid * 128 : grid * 128 + 128]
        for grid in range(2):
            value = line_transform(lines.at[0], stage[grid, 0], stage[grid, 1])
            lig_spec[grid] = value.astype(BF16).astype(F32)

        for grid in range(2):
            real = imag = None
            for c in range(4):
                weight = weight_ref[c]
                lr = lig_spec[grid, c * 32 : c * 32 + 32]
                li = lig_spec[grid, 128 + c * 32 : 128 + c * 32 + 32]
                rr = rec_spec[c * 32 : c * 32 + 32] * weight
                ri = rec_spec[128 + c * 32 : 128 + c * 32 + 32] * weight
                pr = rr * lr + ri * li
                pi = rr * li - ri * lr
                real = pr if real is None else real + pr
                imag = pi if imag is None else imag + pi
            product[grid * 32 : grid * 32 + 32] = real
            product[64 + grid * 32 : 64 + grid * 32 + 32] = imag

        if k == 0:
            loads[4].wait()
            loads[5].wait()
        high, low = split(product[...])
        back[...] = line_transform(back_lines, high, low)
        high, low = split(jnp.concatenate([back[:64], back[64:]], 1))
        both = jnp.concatenate([high, low], 0)
        for tile in range(CELLS // 256):
            part = dot(both, inverse[0, tile])
            total[:, tile * 256 : (tile + 1) * 256] = part[:64] + part[64:] + dot(high, inverse[1, tile])

        pair = [total[:32] * scale, total[32:] * scale]
        for j in range(2):
            value = jnp.where(rotations_ref[0, k, j] == 0, pair[0], pair[1])
            score_v[k, j] = value.astype(BF16)
            top = jnp.where(jnp.logical_and(sub == k, lane == j), jnp.max(value), top)

    out = pltpu.make_async_copy(score_v, scores_ref, out_sem)
    out.start()
    tops_ref[0] = top
    tops[0, 5] = top
    copies = [
        send(tops.at[0, 5], tops.at[0, i], top_send.at[0, i], top_recv.at[0, i], rec=at(-step))
        for i, step in enumerate(WINDOW)
    ]
    for copy in copies:
        copy.wait_recv()
    tops[1, 5] = jnp.max(tops[0], axis=0)
    peers = [at(-5), at(5), over(0), over(-5), over(5)]
    copies = [
        send(tops.at[1, 5], tops.at[1, i], top_send.at[1, i], top_recv.at[1, i], rec=peer)
        for i, peer in enumerate(peers)
    ]
    for copy in copies:
        copy.wait_recv()
    tops_ref[1] = jnp.max(tops[1], axis=0)
    for copy in sent:
        copy.wait_send()
    out.wait()


def write_kernel(scores_in, tops_in, scores_ref, best_ref, best_all_ref, held, in_sem, out_sem):
    reads = [pltpu.make_async_copy(scores_in.at[k], held.at[k], in_sem.at[k]) for k in range(2)]
    writes = [pltpu.make_async_copy(held.at[k], scores_ref.at[k], out_sem.at[k]) for k in range(2)]
    for copy in reads:
        copy.start()
    best_ref[0, 0] = tops_in[0, :2, :2]
    best_all_ref[0] = tops_in[1, :2, :2]
    for k in range(2):
        reads[k].wait()
        writes[k].start()
    for copy in writes:
        copy.wait()


def on_device(receptor, ligand_pool, channel_weight, owners, rotations, n, ligs):
    channels = ligand_pool.shape[3]
    scale = 1.0 / (float(G) ** 3 * float(channels * G**3) ** 0.5)
    forward, inverse, fold = plane_tables()
    lines, back_lines = line_tables()
    own = ligand_pool.reshape(n, 16, CELLS)
    vmem = pl.BlockSpec(memory_space=pltpu.VMEM)
    smem = pl.BlockSpec(memory_space=pltpu.SMEM)
    hbm = pl.BlockSpec(memory_space=pl.ANY)
    dma = pltpu.SemaphoreType.DMA
    scores, tops = pl.pallas_call(
        functools.partial(kernel, n, scale),
        out_shape=(
            jax.ShapeDtypeStruct((2, 2, G, CELLS), BF16),
            jax.ShapeDtypeStruct((2, 8, LANES), F32),
        ),
        in_specs=[vmem, smem, smem, smem, hbm, hbm, hbm, hbm, hbm, hbm],
        out_specs=(hbm, vmem),
        scratch_shapes=[
            pltpu.VMEM((n, 16, CELLS), BF16),
            pltpu.VMEM(forward.shape, BF16),
            pltpu.VMEM(inverse.shape, BF16),
            pltpu.VMEM(lines.shape, BF16),
            pltpu.VMEM(back_lines.shape, BF16),
            pltpu.VMEM(fold.shape, F32),
            pltpu.VMEM((4, 3, 16, CELLS), BF16),
            pltpu.VMEM((2, 16, COLS), BF16),
            pltpu.VMEM((3, 2, 2, 16, COLS), BF16),
            pltpu.VMEM((5, 2, 16, COLS), BF16),
            pltpu.VMEM((2, n, 2, 16, COLS), BF16),
            pltpu.VMEM((ligs, 16, COLS), BF16),
            pltpu.VMEM((2, BLOCKS, 256, 2 * LANES), F32),
            pltpu.VMEM((2, 2, 256, FREQS), BF16),
            pltpu.VMEM((2, 256, FREQS), BF16),
            pltpu.VMEM((256, FREQS), F32),
            pltpu.VMEM((2, 256, FREQS), F32),
            pltpu.VMEM((128, FREQS), F32),
            pltpu.VMEM((128, FREQS), F32),
            pltpu.VMEM((64, CELLS), F32),
            pltpu.VMEM((2, 2, G, CELLS), BF16),
            pltpu.VMEM((2, 6, 8, LANES), F32),
            dma((6,)),
            dma,
            dma((4, 3)),
            dma((4, 3)),
            dma((2,)),
            dma((2,)),
            dma((3, 2, 2)),
            dma((5, 2)),
            dma((6, 2)),
            dma((6, 2)),
            dma((4, 2, 2)),
            dma((4, 2, 2)),
            dma((2,)),
            dma((2,)),
            dma((2, n)),
            dma((2, n)),
            dma((2, 3)),
            dma((2, 3)),
            dma((2, 5)),
            dma((2, 5)),
        ],
        compiler_params=pltpu.CompilerParams(
            collective_id=0, has_side_effects=True, vmem_limit_bytes=56 * 2**20
        ),
        cost_estimate=pl.CostEstimate(flops=6 * 10**9, bytes_accessed=12 * 2**20, transcendentals=0),
    )(receptor[0], channel_weight, owners, rotations, own, forward, inverse, lines, back_lines, fold)
    scores, best, best_all = pl.pallas_call(
        write_kernel,
        out_shape=(
            jax.ShapeDtypeStruct((2, 2, G, CELLS), BF16),
            jax.ShapeDtypeStruct((1, 1, 2, 2), F32),
            jax.ShapeDtypeStruct((1, 2, 2), F32),
        ),
        in_specs=[hbm, vmem],
        out_specs=(hbm, vmem, vmem),
        scratch_shapes=[pltpu.VMEM((2, 2, G, CELLS), BF16), dma((2,)), dma((2,))],
        cost_estimate=pl.CostEstimate(flops=0, bytes_accessed=2**19, transcendentals=0),
    )(scores, tops)
    return scores[None, None], best, best_all


def solution(mesh):
    in_specs = (
        P("rec", None, "lig", None),
        P("lig", "rec", None, None, None, None),
        P(),
        P("lig", None),
        P("lig", None, None),
    )
    out_specs = (
        P("rec", "lig", None, None, None, None),
        P("rec", "lig", None, None),
        P("lig", None, None),
    )
    body = functools.partial(on_device, n=mesh.shape["rec"] // 2, ligs=mesh.shape["lig"])
    return jax.shard_map(body, mesh=mesh, in_specs=in_specs, out_specs=out_specs, check_vma=False)
```

```python
import functools

import jax
import jax.numpy as jnp
import ml_dtypes
import numpy as np
from jax import lax
from jax.experimental import pallas as pl
from jax.experimental.pallas import tpu as pltpu
from jax.sharding import PartitionSpec as P

MESH = pl.DeviceIdType.MESH
G = 32
CELLS = G * G
HALF = G // 2 + 1
LANES = 128
BLOCKS = -(-G * HALF // LANES)
FREQS = BLOCKS * LANES
BF16 = jnp.bfloat16
F32 = jnp.float32


def split_table(table):
    high = table.astype(np.float32).astype(ml_dtypes.bfloat16)
    low = (table - high.astype(np.float64)).astype(np.float32).astype(ml_dtypes.bfloat16)
    return np.stack([high, low], 0)


def plane_tables():
    freq = np.arange(FREQS)
    used = freq < G * HALF
    ky, kz = freq // HALF, freq % HALF
    cell = np.arange(CELLS)
    y, z = cell // G, cell % G
    angle = 2.0 * np.pi * ((y[:, None] * ky + z[:, None] * kz) % G) / G
    cosine = np.where(used, np.cos(angle), 0.0).reshape(CELLS, BLOCKS, LANES)
    sine = np.where(used, np.sin(angle), 0.0).reshape(CELLS, BLOCKS, LANES)
    table = np.stack([cosine, -sine], 2)
    forward = table.transpose(1, 0, 2, 3).reshape(BLOCKS, CELLS, 2 * LANES)
    inverse = table.transpose(2, 1, 3, 0).reshape(2 * FREQS, CELLS // 256, 256).transpose(1, 0, 2)
    weight = np.where(used, np.where((kz == 0) | (kz == G // 2), 1.0, 2.0), 0.0)
    return split_table(forward), split_table(inverse), weight.astype(np.float32).reshape(1, FREQS)


def line_table(rows_in, rows_out, sign):
    group_in, x = rows_in
    group_out, k = rows_out
    angle = 2.0 * np.pi * ((k[:, None] * x[None, :]) % G) / G
    same = group_out[:, None] == group_in[None, :]
    cosine = np.where(same, np.cos(angle), 0.0)
    sine = np.where(same, np.sin(angle), 0.0) * sign
    return split_table(np.block([[cosine, sine], [-sine, cosine]]))


def line_tables():
    row = np.arange(128)
    plain = (row // G, row % G)
    rec = ((row // 2) % 4, (row // 8) * 2 + row % 2)
    pair = (plain[0][:64], plain[1][:64])
    forward = np.stack([line_table(plain, plain, 1.0), line_table(rec, plain, 1.0)], 0)
    return forward, line_table(pair, pair, -1.0)


def dot(a, b):
    return jnp.dot(a, b, preferred_element_type=F32)


def split(value):
    high = value.astype(BF16)
    return high, (value - high.astype(F32)).astype(BF16)


def line_transform(table, high, low):
    return dot(table[0], high) + dot(table[0], low) + dot(table[1], high)


def half_plane(data, forward, block, half):
    rows = pl.ds(pl.multiple_of(half * COLS, COLS), COLS)
    return dot(data, forward[0, block, rows]) + dot(data, forward[1, block, rows])


NEAR = (-2, -1, 1, 2)
FAR = (-5, 5)
COLS = CELLS // 2


def kernel(
    n,
    scale,
    rec_ref,
    weight_ref,
    owners_ref,
    rotations_ref,
    own_hbm,
    forward_hbm,
    inverse_hbm,
    lines_hbm,
    back_hbm,
    fold_hbm,
    scores_ref,
    tops_ref,
    own,
    forward,
    inverse,
    lines,
    back_lines,
    fold,
    leaves,
    ends,
    partial,
    roots,
    gathered,
    rec_all,
    sums,
    stage,
    rec_stage,
    rec_spec,
    lig_spec,
    product,
    back,
    total,
    score_v,
    tops,
    table_sem,
    out_sem,
    leaf_send,
    leaf_recv,
    end_send,
    end_recv,
    root_send,
    root_recv,
    first_send,
    first_recv,
    relay_send,
    relay_recv,
    last_send,
    last_recv,
    cross_send,
    cross_recv,
    rec_send,
    rec_recv,
    top_send,
    top_recv,
):
    rec = lax.axis_index("rec")
    lig = lax.axis_index("lig")
    side = rec // n
    me = lax.rem(rec, n)
    partner = lax.rem(rec + n, 2 * n)

    def shift(step):
        return lax.rem(me + n + step, n)

    def at(step):
        return side * n + shift(step)

    def over(step):
        return (1 - side) * n + shift(step)

    quad = lig // 4
    quad_peers = [quad * 4 + lax.rem(lig + step, 4) for step in range(1, 4)]
    line_peers = [lax.rem(lig + 4 * step, 16) for step in range(1, 4)]

    barrier = pltpu.get_barrier_semaphore()
    rec_peers = [over(step) for step in (-2, 2)] + [at(step) for step in (-3, 3, -2, 2, -1, 1)] + [over(0)]
    for peer in rec_peers:
        pl.semaphore_signal(barrier, inc=1, device_id={"rec": peer}, device_id_type=MESH)
    for peer in quad_peers + line_peers:
        pl.semaphore_signal(barrier, inc=1, device_id={"lig": peer}, device_id_type=MESH)

    loads = [
        pltpu.make_async_copy(src, dst, table_sem.at[i])
        for i, (src, dst) in enumerate(
            [(own_hbm, own), (forward_hbm, forward), (lines_hbm, lines), (fold_hbm, fold), (inverse_hbm, inverse), (back_hbm, back_lines)]
        )
    ]
    for copy in loads:
        copy.start()

    slab = jnp.concatenate([rec_ref[c].astype(F32) for c in range(4)], 0)
    rec_all[lig] = jnp.concatenate([slab[:, :COLS], slab[:, COLS:]], 0).astype(BF16)
    loads[0].wait()
    pl.semaphore_wait(barrier, len(rec_peers) + 6)

    sent = []

    def send(src, dst, send_sem, recv_sem, **where):
        copy = pltpu.make_async_remote_copy(
            src_ref=src,
            dst_ref=dst,
            send_sem=send_sem,
            recv_sem=recv_sem,
            device_id=where,
            device_id_type=MESH,
        )
        copy.start()
        sent.append(copy)
        return copy

    owner = [owners_ref[0, k] for k in range(2)]
    owner_z = [lax.rem(owner[k], n) for k in range(2)]
    owner_side = [owner[k] // n for k in range(2)]

    far = shift(n // 2)
    end = [
        send(own.at[far, :, :COLS], ends.at[0], end_send.at[0], end_recv.at[0], rec=at(-3)),
        send(own.at[far, :, COLS:], ends.at[1], end_send.at[1], end_recv.at[1], rec=at(3)),
    ]
    leaf = {}
    for j, step in ((1, -5), (2, 5), (0, 0)):
        for i, to in enumerate(NEAR):
            leaf[i, j] = send(
                own.at[shift(to + step)], leaves.at[i, j], leaf_send.at[i, j], leaf_recv.at[i, j], rec=at(to)
            )
    slabs = [
        send(rec_all.at[lig], rec_all.at[lig], rec_send.at[0, i], rec_recv.at[0, i], lig=peer)
        for i, peer in enumerate(quad_peers)
    ]
    for copy in slabs:
        copy.wait_recv()
    block = rec_all.at[pl.ds(quad * 4, 4)]
    slabs = [
        send(block, block, rec_send.at[1, i], rec_recv.at[1, i], lig=peer) for i, peer in enumerate(line_peers)
    ]

    for copy in end:
        copy.wait_recv()
    root = {}
    for j, step in ((1, -5), (2, 5), (0, 0)):
        shard = shift(step)
        for i in range(len(NEAR)):
            leaf[i, j].wait_recv()
        for k in range(2):
            away = lax.rem(owner_z[k] - me + n, n)
            value = own[shard]
            for i, to in enumerate(NEAR):
                value = jnp.where(away == (n - to) % n, leaves[i, j], value)
            parts = [value[:, :COLS], value[:, COLS:]]
            if j == 1:
                parts[0] = jnp.where(away == 3, ends[0], parts[0])
            if j == 2:
                parts[1] = jnp.where(away == n - 3, ends[1], parts[1])
            for half in range(2):
                partial[j, half, k] = parts[half]
            if j:
                for half in range(2):
                    slot = (j - 1) * 2 + side
                    root[j, half, k] = send(
                        partial.at[j, half, k],
                        roots.at[slot, k],
                        root_send.at[j - 1, half, k],
                        root_recv.at[slot, k],
                        rec=half * n + shard,
                    )
            else:
                root[0, k] = send(
                    partial.at[0, 1 - side, k],
                    roots.at[4, k],
                    root_send.at[2, 0, k],
                    root_recv.at[4, k],
                    rec=partner,
                )

    for copy in slabs:
        copy.wait_recv()
    loads[1].wait()
    loads[2].wait()
    loads[3].wait()
    grid = rec_all[...].astype(F32)
    rows = [grid[:, half * 8 : half * 8 + 8].reshape(128, COLS).astype(BF16) for half in range(2)]
    for block in range(BLOCKS):
        lanes = pl.ds(block * LANES, LANES)
        value = half_plane(rows[0], forward, block, 0) + half_plane(rows[1], forward, block, 1)
        for part in range(2):
            high, low = split(value[:, part * LANES : (part + 1) * LANES])
            rec_stage[0, part * 128 : (part + 1) * 128, lanes] = high
            rec_stage[1, part * 128 : (part + 1) * 128, lanes] = low
    rec_spec[...] = line_transform(lines.at[1], rec_stage[0], rec_stage[1]) * fold[...]

    def root_wait(slot, k):
        pltpu.make_async_copy(roots.at[slot, k], roots.at[slot, k], root_recv.at[slot, k]).wait()

    first, relay, last = {}, {}, {}
    cross = [[], []]

    def spread(k, shard):
        ref = gathered.at[k, shard, side]
        slot = len(cross[k])
        cross[k].append(send(ref, ref, cross_send.at[k, slot], cross_recv.at[k, slot], rec=partner))

    def gather_first(k):
        for slot in range(5):
            root_wait(slot, k)
        away = lax.rem(owner_z[k] - me + n, n)
        below = jnp.logical_or(away > n // 2, jnp.logical_and(away == n // 2, side == 1))
        inner = jnp.logical_or(away <= 2, away >= n - 2)
        here = owner_side[k] == side
        middle = jnp.where(here, partial[0, side, k], roots[4, k])
        up = jnp.where(owner_side[k] == 0, roots[0, k], roots[1, k])
        down = jnp.where(owner_side[k] == 0, roots[2, k], roots[3, k])
        gathered[k, me, side] = jnp.where(inner, middle, jnp.where(below, down, up))
        mine = gathered.at[k, me, side]
        for i, to in enumerate(FAR + NEAR):
            first[k, to] = send(mine, mine, first_send.at[i, k], first_recv.at[i, k], rec=at(to))
        spread(k, me)

    def gather_relay(k):
        for j, to in enumerate(FAR):
            first[k, to].wait_recv()
            shard = shift(-to)
            ref = gathered.at[k, shard, side]
            for i, near in enumerate(NEAR):
                relay[i, j, k] = send(ref, ref, relay_send.at[i, j, k], relay_recv.at[i, j, k], rec=at(near))
            if j == k:
                last[k] = send(ref, ref, last_send.at[k], last_recv.at[k], rec=at(-3 if to < 0 else 3))
            spread(k, shard)
        for to in NEAR:
            first[k, to].wait_recv()
            spread(k, shift(-to))

    def gather_cross(k):
        for j, to in enumerate(FAR):
            for i, near in enumerate(NEAR):
                relay[i, j, k].wait_recv()
                spread(k, shift(-near - to))
        last[k].wait_recv()
        spread(k, far)

    for k in range(2):
        gather_first(k)
    for k in range(2):
        gather_relay(k)
    for k in range(2):
        gather_cross(k)

    def half_rows(k, half):
        return gathered[k, :, half].reshape(256, COLS)

    for k in range(2):
        data = half_rows(k, side)
        for block in range(BLOCKS):
            sums[k, block] = half_plane(data, forward, block, side)

    sub = lax.broadcasted_iota(jnp.int32, (8, LANES), 0)
    lane = lax.broadcasted_iota(jnp.int32, (8, LANES), 1)
    top = jnp.zeros((8, LANES), F32)
    for k in range(2):
        for copy in cross[k]:
            copy.wait_recv()

        data = half_rows(k, 1 - side)
        for block in range(BLOCKS):
            lanes = pl.ds(block * LANES, LANES)
            value = sums[k, block] + half_plane(data, forward, block, 1 - side)
            for part in range(2):
                high, low = split(value[:, part * LANES : (part + 1) * LANES])
                for grid in range(2):
                    stage[grid, 0, part * 128 : (part + 1) * 128, lanes] = high[grid * 128 : grid * 128 + 128]
                    stage[grid, 1, part * 128 : (part + 1) * 128, lanes] = low[grid * 128 : grid * 128 + 128]
        for grid in range(2):
            value = line_transform(lines.at[0], stage[grid, 0], stage[grid, 1])
            lig_spec[grid] = value.astype(BF16).astype(F32)

        for grid in range(2):
            real = imag = None
            for c in range(4):
                weight = weight_ref[c]
                lr = lig_spec[grid, c * 32 : c * 32 + 32]
                li = lig_spec[grid, 128 + c * 32 : 128 + c * 32 + 32]
                rr = rec_spec[c * 32 : c * 32 + 32] * weight
                ri = rec_spec[128 + c * 32 : 128 + c * 32 + 32] * weight
                pr = rr * lr + ri * li
                pi = rr * li - ri * lr
                real = pr if real is None else real + pr
                imag = pi if imag is None else imag + pi
            product[grid * 32 : grid * 32 + 32] = real
            product[64 + grid * 32 : 64 + grid * 32 + 32] = imag

        if k == 0:
            loads[4].wait()
            loads[5].wait()
        high, low = split(product[...])
        back[...] = line_transform(back_lines, high, low)
        high, low = split(jnp.concatenate([back[:64], back[64:]], 1))
        both = jnp.concatenate([high, low], 0)
        for tile in range(CELLS // 256):
            part = dot(both, inverse[0, tile])
            total[:, tile * 256 : (tile + 1) * 256] = part[:64] + part[64:] + dot(high, inverse[1, tile])

        pair = [total[:32] * scale, total[32:] * scale]
        for j in range(2):
            value = jnp.where(rotations_ref[0, k, j] == 0, pair[0], pair[1])
            score_v[k, j] = value.astype(BF16)
            top = jnp.where(jnp.logical_and(sub == k, lane == j), jnp.max(value), top)

    out = pltpu.make_async_copy(score_v, scores_ref, out_sem)
    out.start()
    tops_ref[0] = top
    tops[0] = top
    steps = sorted(range(1, n), key=lambda step: -min(step, n - step))
    peers = [over(step) for step in steps[:7]] + [at(step) for step in steps[:7]]
    peers += [over(step) for step in steps[7:]] + [at(step) for step in steps[7:]] + [over(0)]
    copies = [
        send(tops.at[0], tops.at[1 + i], top_send.at[i], top_recv.at[i], rec=peer) for i, peer in enumerate(peers)
    ]
    for copy in copies:
        copy.wait_recv()
    tops_ref[1] = jnp.max(tops[...], axis=0)
    for copy in sent:
        copy.wait_send()
    out.wait()


def write_kernel(scores_in, tops_in, scores_ref, best_ref, best_all_ref, held, in_sem, out_sem):
    reads = [pltpu.make_async_copy(scores_in.at[k], held.at[k], in_sem.at[k]) for k in range(2)]
    writes = [pltpu.make_async_copy(held.at[k], scores_ref.at[k], out_sem.at[k]) for k in range(2)]
    for copy in reads:
        copy.start()
    best_ref[0, 0] = tops_in[0, :2, :2]
    best_all_ref[0] = tops_in[1, :2, :2]
    for k in range(2):
        reads[k].wait()
        writes[k].start()
    for copy in writes:
        copy.wait()


def on_device(receptor, ligand_pool, channel_weight, owners, rotations, n, ligs):
    channels = ligand_pool.shape[3]
    scale = 1.0 / (float(G) ** 3 * float(channels * G**3) ** 0.5)
    forward, inverse, fold = plane_tables()
    lines, back_lines = line_tables()
    own = ligand_pool.reshape(n, 16, CELLS)
    vmem = pl.BlockSpec(memory_space=pltpu.VMEM)
    smem = pl.BlockSpec(memory_space=pltpu.SMEM)
    hbm = pl.BlockSpec(memory_space=pl.ANY)
    dma = pltpu.SemaphoreType.DMA
    scores, tops = pl.pallas_call(
        functools.partial(kernel, n, scale),
        out_shape=(
            jax.ShapeDtypeStruct((2, 2, G, CELLS), BF16),
            jax.ShapeDtypeStruct((2, 8, LANES), F32),
        ),
        in_specs=[vmem, smem, smem, smem, hbm, hbm, hbm, hbm, hbm, hbm],
        out_specs=(hbm, vmem),
        scratch_shapes=[
            pltpu.VMEM((n, 16, CELLS), BF16),
            pltpu.VMEM(forward.shape, BF16),
            pltpu.VMEM(inverse.shape, BF16),
            pltpu.VMEM(lines.shape, BF16),
            pltpu.VMEM(back_lines.shape, BF16),
            pltpu.VMEM(fold.shape, F32),
            pltpu.VMEM((4, 3, 16, CELLS), BF16),
            pltpu.VMEM((2, 16, COLS), BF16),
            pltpu.VMEM((3, 2, 2, 16, COLS), BF16),
            pltpu.VMEM((5, 2, 16, COLS), BF16),
            pltpu.VMEM((2, n, 2, 16, COLS), BF16),
            pltpu.VMEM((ligs, 16, COLS), BF16),
            pltpu.VMEM((2, BLOCKS, 256, 2 * LANES), F32),
            pltpu.VMEM((2, 2, 256, FREQS), BF16),
            pltpu.VMEM((2, 256, FREQS), BF16),
            pltpu.VMEM((256, FREQS), F32),
            pltpu.VMEM((2, 256, FREQS), F32),
            pltpu.VMEM((128, FREQS), F32),
            pltpu.VMEM((128, FREQS), F32),
            pltpu.VMEM((64, CELLS), F32),
            pltpu.VMEM((2, 2, G, CELLS), BF16),
            pltpu.VMEM((2 * n, 8, LANES), F32),
            dma((6,)),
            dma,
            dma((4, 3)),
            dma((4, 3)),
            dma((2,)),
            dma((2,)),
            dma((3, 2, 2)),
            dma((5, 2)),
            dma((6, 2)),
            dma((6, 2)),
            dma((4, 2, 2)),
            dma((4, 2, 2)),
            dma((2,)),
            dma((2,)),
            dma((2, n)),
            dma((2, n)),
            dma((2, 3)),
            dma((2, 3)),
            dma((2 * n - 1,)),
            dma((2 * n - 1,)),
        ],
        compiler_params=pltpu.CompilerParams(
            collective_id=0, has_side_effects=True, vmem_limit_bytes=56 * 2**20
        ),
        cost_estimate=pl.CostEstimate(flops=6 * 10**9, bytes_accessed=12 * 2**20, transcendentals=0),
    )(receptor[0], channel_weight, owners, rotations, own, forward, inverse, lines, back_lines, fold)
    scores, best, best_all = pl.pallas_call(
        write_kernel,
        out_shape=(
            jax.ShapeDtypeStruct((2, 2, G, CELLS), BF16),
            jax.ShapeDtypeStruct((1, 1, 2, 2), F32),
            jax.ShapeDtypeStruct((1, 2, 2), F32),
        ),
        in_specs=[hbm, vmem],
        out_specs=(hbm, vmem, vmem),
        scratch_shapes=[pltpu.VMEM((2, 2, G, CELLS), BF16), dma((2,)), dma((2,))],
        cost_estimate=pl.CostEstimate(flops=0, bytes_accessed=2**19, transcendentals=0),
    )(scores, tops)
    return scores[None, None], best, best_all


def solution(mesh):
    in_specs = (
        P("rec", None, "lig", None),
        P("lig", "rec", None, None, None, None),
        P(),
        P("lig", None),
        P("lig", None, None),
    )
    out_specs = (
        P("rec", "lig", None, None, None, None),
        P("rec", "lig", None, None),
        P("lig", None, None),
    )
    body = functools.partial(on_device, n=mesh.shape["rec"] // 2, ligs=mesh.shape["lig"])
    return jax.shard_map(body, mesh=mesh, in_specs=in_specs, out_specs=out_specs, check_vma=False)
```

```python
import functools

import jax
import jax.numpy as jnp
import ml_dtypes
import numpy as np
from jax import lax
from jax.experimental import pallas as pl
from jax.experimental.pallas import tpu as pltpu
from jax.sharding import PartitionSpec as P

MESH = pl.DeviceIdType.MESH
G = 32
CELLS = G * G
HALF = G // 2 + 1
LANES = 128
BLOCKS = -(-G * HALF // LANES)
FREQS = BLOCKS * LANES
BF16 = jnp.bfloat16
F32 = jnp.float32


def split_table(table):
    high = table.astype(np.float32).astype(ml_dtypes.bfloat16)
    low = (table - high.astype(np.float64)).astype(np.float32).astype(ml_dtypes.bfloat16)
    return np.stack([high, low], 0)


def plane_tables():
    freq = np.arange(FREQS)
    used = freq < G * HALF
    ky, kz = freq // HALF, freq % HALF
    cell = np.arange(CELLS)
    y, z = cell // G, cell % G
    angle = 2.0 * np.pi * ((y[:, None] * ky + z[:, None] * kz) % G) / G
    cosine = np.where(used, np.cos(angle), 0.0).reshape(CELLS, BLOCKS, LANES)
    sine = np.where(used, np.sin(angle), 0.0).reshape(CELLS, BLOCKS, LANES)
    table = np.stack([cosine, -sine], 2)
    forward = table.transpose(1, 0, 2, 3).reshape(BLOCKS, CELLS, 2 * LANES)
    inverse = table.transpose(2, 1, 3, 0).reshape(2 * FREQS, CELLS // 256, 256).transpose(1, 0, 2)
    weight = np.where(used, np.where((kz == 0) | (kz == G // 2), 1.0, 2.0), 0.0)
    return split_table(forward), split_table(inverse), weight.astype(np.float32).reshape(1, FREQS)


def line_table(rows_in, rows_out, sign):
    group_in, x = rows_in
    group_out, k = rows_out
    angle = 2.0 * np.pi * ((k[:, None] * x[None, :]) % G) / G
    same = group_out[:, None] == group_in[None, :]
    cosine = np.where(same, np.cos(angle), 0.0)
    sine = np.where(same, np.sin(angle), 0.0) * sign
    return split_table(np.block([[cosine, sine], [-sine, cosine]]))


def line_tables():
    row = np.arange(128)
    plain = (row // G, row % G)
    rec = ((row // 2) % 4, (row // 8) * 2 + row % 2)
    pair = (plain[0][:64], plain[1][:64])
    forward = np.stack([line_table(plain, plain, 1.0), line_table(rec, plain, 1.0)], 0)
    return forward, line_table(pair, pair, -1.0)


def dot(a, b):
    return jnp.dot(a, b, preferred_element_type=F32)


def split(value):
    high = value.astype(BF16)
    return high, (value - high.astype(F32)).astype(BF16)


def line_transform(table, high, low):
    return dot(table[0], high) + dot(table[0], low) + dot(table[1], high)


def half_plane(data, forward, block, half):
    rows = pl.ds(pl.multiple_of(half * COLS, COLS), COLS)
    return dot(data, forward[0, block, rows]) + dot(data, forward[1, block, rows])


NEAR = (-2, -1, 1, 2)
FAR = (-5, 5)
COLS = CELLS // 2


def kernel(
    n,
    scale,
    rec_hbm,
    weight_hbm,
    owners_hbm,
    rotations_hbm,
    own_hbm,
    forward_hbm,
    inverse_hbm,
    lines_hbm,
    back_hbm,
    fold_hbm,
    scores_ref,
    tops_ref,
    rec_ref,
    weight_ref,
    owners_ref,
    rotations_ref,
    own,
    forward,
    inverse,
    lines,
    back_lines,
    fold,
    leaves,
    ends,
    partial,
    roots,
    gathered,
    rec_all,
    sums,
    stage,
    rec_stage,
    rec_spec,
    lig_spec,
    product,
    back,
    total,
    score_v,
    tops,
    small_sem,
    table_sem,
    out_sem,
    leaf_send,
    leaf_recv,
    end_send,
    end_recv,
    root_send,
    root_recv,
    first_send,
    first_recv,
    relay_send,
    relay_recv,
    last_send,
    last_recv,
    cross_send,
    cross_recv,
    rec_send,
    rec_recv,
    top_send,
    top_recv,
):
    rec = lax.axis_index("rec")
    lig = lax.axis_index("lig")
    side = rec // n
    me = lax.rem(rec, n)
    partner = lax.rem(rec + n, 2 * n)

    def shift(step):
        return lax.rem(me + n + step, n)

    def at(step):
        return side * n + shift(step)

    def over(step):
        return (1 - side) * n + shift(step)

    quad = lig // 4
    quad_peers = [quad * 4 + lax.rem(lig + step, 4) for step in range(1, 4)]
    line_peers = [lax.rem(lig + 4 * step, 16) for step in range(1, 4)]

    barrier = pltpu.get_barrier_semaphore()
    rec_peers = [over(step) for step in (-2, 2)] + [at(step) for step in (-3, 3, -2, 2, -1, 1)] + [over(0)]
    for peer in rec_peers:
        pl.semaphore_signal(barrier, inc=1, device_id={"rec": peer}, device_id_type=MESH)
    for peer in quad_peers + line_peers:
        pl.semaphore_signal(barrier, inc=1, device_id={"lig": peer}, device_id_type=MESH)

    small = [
        pltpu.make_async_copy(src, dst, small_sem.at[i])
        for i, (src, dst) in enumerate(
            [(rec_hbm, rec_ref), (owners_hbm, owners_ref), (rotations_hbm, rotations_ref), (weight_hbm, weight_ref)]
        )
    ]
    small[0].start()
    loads = [
        pltpu.make_async_copy(src, dst, table_sem.at[i])
        for i, (src, dst) in enumerate(
            [(own_hbm, own), (forward_hbm, forward), (lines_hbm, lines), (fold_hbm, fold), (inverse_hbm, inverse), (back_hbm, back_lines)]
        )
    ]
    loads[0].start()
    for copy in small[1:] + loads[1:]:
        copy.start()
    small[0].wait()

    slab = jnp.concatenate([rec_ref[c].astype(F32) for c in range(4)], 0)
    rec_all[lig] = jnp.concatenate([slab[:, :COLS], slab[:, COLS:]], 0).astype(BF16)
    for copy in [loads[0]] + small[1:]:
        copy.wait()
    pl.semaphore_wait(barrier, len(rec_peers) + 6)

    sent = []

    def send(src, dst, send_sem, recv_sem, **where):
        copy = pltpu.make_async_remote_copy(
            src_ref=src,
            dst_ref=dst,
            send_sem=send_sem,
            recv_sem=recv_sem,
            device_id=where,
            device_id_type=MESH,
        )
        copy.start()
        sent.append(copy)
        return copy

    owner = [owners_ref[0, k] for k in range(2)]
    owner_z = [lax.rem(owner[k], n) for k in range(2)]
    owner_side = [owner[k] // n for k in range(2)]

    far = shift(n // 2)
    end = [
        send(own.at[far, :, :COLS], ends.at[0], end_send.at[0], end_recv.at[0], rec=at(-3)),
        send(own.at[far, :, COLS:], ends.at[1], end_send.at[1], end_recv.at[1], rec=at(3)),
    ]
    leaf = {}
    for j, step in ((1, -5), (2, 5), (0, 0)):
        for i, to in enumerate(NEAR):
            leaf[i, j] = send(
                own.at[shift(to + step)], leaves.at[i, j], leaf_send.at[i, j], leaf_recv.at[i, j], rec=at(to)
            )
    slabs = [
        send(rec_all.at[lig], rec_all.at[lig], rec_send.at[0, i], rec_recv.at[0, i], lig=peer)
        for i, peer in enumerate(quad_peers)
    ]
    for copy in slabs:
        copy.wait_recv()
    block = rec_all.at[pl.ds(quad * 4, 4)]
    slabs = [
        send(block, block, rec_send.at[1, i], rec_recv.at[1, i], lig=peer) for i, peer in enumerate(line_peers)
    ]

    for copy in end:
        copy.wait_recv()
    root = {}
    for j, step in ((1, -5), (2, 5), (0, 0)):
        shard = shift(step)
        for i in range(len(NEAR)):
            leaf[i, j].wait_recv()
        for k in range(2):
            away = lax.rem(owner_z[k] - me + n, n)
            value = own[shard]
            for i, to in enumerate(NEAR):
                value = jnp.where(away == (n - to) % n, leaves[i, j], value)
            parts = [value[:, :COLS], value[:, COLS:]]
            if j == 1:
                parts[0] = jnp.where(away == 3, ends[0], parts[0])
            if j == 2:
                parts[1] = jnp.where(away == n - 3, ends[1], parts[1])
            for half in range(2):
                partial[j, half, k] = parts[half]
            if j:
                for half in range(2):
                    slot = (j - 1) * 2 + side
                    root[j, half, k] = send(
                        partial.at[j, half, k],
                        roots.at[slot, k],
                        root_send.at[j - 1, half, k],
                        root_recv.at[slot, k],
                        rec=half * n + shard,
                    )
            else:
                root[0, k] = send(
                    partial.at[0, 1 - side, k],
                    roots.at[4, k],
                    root_send.at[2, 0, k],
                    root_recv.at[4, k],
                    rec=partner,
                )

    for copy in slabs:
        copy.wait_recv()
    loads[1].wait()
    loads[2].wait()
    loads[3].wait()
    grid = rec_all[...].astype(F32)
    rows = [grid[:, half * 8 : half * 8 + 8].reshape(128, COLS).astype(BF16) for half in range(2)]
    for block in range(BLOCKS):
        lanes = pl.ds(block * LANES, LANES)
        value = half_plane(rows[0], forward, block, 0) + half_plane(rows[1], forward, block, 1)
        for part in range(2):
            high, low = split(value[:, part * LANES : (part + 1) * LANES])
            rec_stage[0, part * 128 : (part + 1) * 128, lanes] = high
            rec_stage[1, part * 128 : (part + 1) * 128, lanes] = low
    rec_spec[...] = line_transform(lines.at[1], rec_stage[0], rec_stage[1]) * fold[...]

    def root_wait(slot, k):
        pltpu.make_async_copy(roots.at[slot, k], roots.at[slot, k], root_recv.at[slot, k]).wait()

    first, relay, last = {}, {}, {}
    cross = [[], []]

    def spread(k, shard):
        ref = gathered.at[k, shard, side]
        slot = len(cross[k])
        cross[k].append(send(ref, ref, cross_send.at[k, slot], cross_recv.at[k, slot], rec=partner))

    def gather_first(k):
        for slot in range(5):
            root_wait(slot, k)
        away = lax.rem(owner_z[k] - me + n, n)
        below = jnp.logical_or(away > n // 2, jnp.logical_and(away == n // 2, side == 1))
        inner = jnp.logical_or(away <= 2, away >= n - 2)
        here = owner_side[k] == side
        middle = jnp.where(here, partial[0, side, k], roots[4, k])
        up = jnp.where(owner_side[k] == 0, roots[0, k], roots[1, k])
        down = jnp.where(owner_side[k] == 0, roots[2, k], roots[3, k])
        gathered[k, me, side] = jnp.where(inner, middle, jnp.where(below, down, up))
        mine = gathered.at[k, me, side]
        for i, to in enumerate(FAR + NEAR):
            first[k, to] = send(mine, mine, first_send.at[i, k], first_recv.at[i, k], rec=at(to))
        spread(k, me)

    def gather_relay(k):
        for j, to in enumerate(FAR):
            first[k, to].wait_recv()
            shard = shift(-to)
            ref = gathered.at[k, shard, side]
            for i, near in enumerate(NEAR):
                relay[i, j, k] = send(ref, ref, relay_send.at[i, j, k], relay_recv.at[i, j, k], rec=at(near))
            if j == k:
                last[k] = send(ref, ref, last_send.at[k], last_recv.at[k], rec=at(-3 if to < 0 else 3))
            spread(k, shard)
        for to in NEAR:
            first[k, to].wait_recv()
            spread(k, shift(-to))

    def gather_cross(k):
        for j, to in enumerate(FAR):
            for i, near in enumerate(NEAR):
                relay[i, j, k].wait_recv()
                spread(k, shift(-near - to))
        last[k].wait_recv()
        spread(k, far)

    for k in range(2):
        gather_first(k)
    for k in range(2):
        gather_relay(k)
    def half_rows(k, half):
        return gathered[k, :, half].reshape(256, COLS)

    for k in range(2):
        gather_cross(k)
        data = half_rows(k, side)
        for block in range(BLOCKS):
            sums[k, block] = half_plane(data, forward, block, side)

    sub = lax.broadcasted_iota(jnp.int32, (8, LANES), 0)
    lane = lax.broadcasted_iota(jnp.int32, (8, LANES), 1)
    top = jnp.zeros((8, LANES), F32)
    for k in range(2):
        for copy in cross[k]:
            copy.wait_recv()

        data = half_rows(k, 1 - side)
        for block in range(BLOCKS):
            lanes = pl.ds(block * LANES, LANES)
            value = sums[k, block] + half_plane(data, forward, block, 1 - side)
            for part in range(2):
                high, low = split(value[:, part * LANES : (part + 1) * LANES])
                for grid in range(2):
                    stage[grid, 0, part * 128 : (part + 1) * 128, lanes] = high[grid * 128 : grid * 128 + 128]
                    stage[grid, 1, part * 128 : (part + 1) * 128, lanes] = low[grid * 128 : grid * 128 + 128]
        for grid in range(2):
            value = line_transform(lines.at[0], stage[grid, 0], stage[grid, 1])
            lig_spec[grid] = value.astype(BF16).astype(F32)

        for grid in range(2):
            real = imag = None
            for c in range(4):
                weight = weight_ref[c]
                lr = lig_spec[grid, c * 32 : c * 32 + 32]
                li = lig_spec[grid, 128 + c * 32 : 128 + c * 32 + 32]
                rr = rec_spec[c * 32 : c * 32 + 32] * weight
                ri = rec_spec[128 + c * 32 : 128 + c * 32 + 32] * weight
                pr = rr * lr + ri * li
                pi = rr * li - ri * lr
                real = pr if real is None else real + pr
                imag = pi if imag is None else imag + pi
            product[grid * 32 : grid * 32 + 32] = real
            product[64 + grid * 32 : 64 + grid * 32 + 32] = imag

        if k == 0:
            loads[4].wait()
            loads[5].wait()
        high, low = split(product[...])
        back[...] = line_transform(back_lines, high, low)
        high, low = split(jnp.concatenate([back[:64], back[64:]], 1))
        both = jnp.concatenate([high, low], 0)
        for tile in range(CELLS // 256):
            part = dot(both, inverse[0, tile])
            total[:, tile * 256 : (tile + 1) * 256] = part[:64] + part[64:] + dot(high, inverse[1, tile])

        pair = [total[:32] * scale, total[32:] * scale]
        for j in range(2):
            value = jnp.where(rotations_ref[0, k, j] == 0, pair[0], pair[1])
            score_v[k, j] = value.astype(BF16)
            top = jnp.where(jnp.logical_and(sub == k, lane == j), jnp.max(value), top)

    earlier = list(sent)
    tops[0] = top
    steps = sorted(range(1, n), key=lambda step: -min(step, n - step))
    peers = [over(step) for step in steps[:7]] + [at(step) for step in steps[:7]]
    peers += [over(step) for step in steps[7:]] + [at(step) for step in steps[7:]] + [over(0)]
    copies = [
        send(tops.at[0], tops.at[1 + i], top_send.at[i], top_recv.at[i], rec=peer) for i, peer in enumerate(peers)
    ]
    out = pltpu.make_async_copy(score_v, scores_ref, out_sem)
    out.start()
    tops_ref[0] = top
    for copy in earlier:
        copy.wait_send()
    out.wait()
    for copy in copies:
        copy.wait_recv()
    tops_ref[1] = jnp.max(tops[...], axis=0)
    for copy in copies:
        copy.wait_send()


def write_kernel(scores_in, tops_in, scores_ref, best_ref, best_all_ref, held, tops, best, best_all, in_sem, out_sem):
    reads = [pltpu.make_async_copy(tops_in, tops, in_sem.at[2])]
    reads += [pltpu.make_async_copy(scores_in.at[k], held.at[k], in_sem.at[k]) for k in range(2)]
    writes = [pltpu.make_async_copy(held.at[k], scores_ref.at[k], out_sem.at[k]) for k in range(2)]
    writes.append(pltpu.make_async_copy(best, best_ref, out_sem.at[2]))
    writes.append(pltpu.make_async_copy(best_all, best_all_ref, out_sem.at[3]))
    for copy in reads:
        copy.start()
    reads[0].wait()
    best[0, 0] = tops[0, :2, :2]
    best_all[0] = tops[1, :2, :2]
    for copy in writes[2:]:
        copy.start()
    for k in range(2):
        reads[1 + k].wait()
        writes[k].start()
    for copy in writes:
        copy.wait()


def on_device(receptor, ligand_pool, channel_weight, owners, rotations, n, ligs):
    channels = ligand_pool.shape[3]
    scale = 1.0 / (float(G) ** 3 * float(channels * G**3) ** 0.5)
    forward, inverse, fold = plane_tables()
    lines, back_lines = line_tables()
    own = ligand_pool.reshape(n, 16, CELLS)
    vmem = pl.BlockSpec(memory_space=pltpu.VMEM)
    hbm = pl.BlockSpec(memory_space=pl.ANY)
    dma = pltpu.SemaphoreType.DMA
    scores, tops = pl.pallas_call(
        functools.partial(kernel, n, scale),
        out_shape=(
            jax.ShapeDtypeStruct((2, 2, G, CELLS), BF16),
            jax.ShapeDtypeStruct((2, 8, LANES), F32),
        ),
        in_specs=[hbm] * 10,
        out_specs=(hbm, vmem),
        scratch_shapes=[
            pltpu.VMEM((channels, 2, CELLS), BF16),
            pltpu.SMEM((channels,), F32),
            pltpu.SMEM(owners.shape, jnp.int32),
            pltpu.SMEM(rotations.shape, jnp.int32),
            pltpu.VMEM((n, 16, CELLS), BF16),
            pltpu.VMEM(forward.shape, BF16),
            pltpu.VMEM(inverse.shape, BF16),
            pltpu.VMEM(lines.shape, BF16),
            pltpu.VMEM(back_lines.shape, BF16),
            pltpu.VMEM(fold.shape, F32),
            pltpu.VMEM((4, 3, 16, CELLS), BF16),
            pltpu.VMEM((2, 16, COLS), BF16),
            pltpu.VMEM((3, 2, 2, 16, COLS), BF16),
            pltpu.VMEM((5, 2, 16, COLS), BF16),
            pltpu.VMEM((2, n, 2, 16, COLS), BF16),
            pltpu.VMEM((ligs, 16, COLS), BF16),
            pltpu.VMEM((2, BLOCKS, 256, 2 * LANES), F32),
            pltpu.VMEM((2, 2, 256, FREQS), BF16),
            pltpu.VMEM((2, 256, FREQS), BF16),
            pltpu.VMEM((256, FREQS), F32),
            pltpu.VMEM((2, 256, FREQS), F32),
            pltpu.VMEM((128, FREQS), F32),
            pltpu.VMEM((128, FREQS), F32),
            pltpu.VMEM((64, CELLS), F32),
            pltpu.VMEM((2, 2, G, CELLS), BF16),
            pltpu.VMEM((2 * n, 8, LANES), F32),
            dma((4,)),
            dma((6,)),
            dma,
            dma((4, 3)),
            dma((4, 3)),
            dma((2,)),
            dma((2,)),
            dma((3, 2, 2)),
            dma((5, 2)),
            dma((6, 2)),
            dma((6, 2)),
            dma((4, 2, 2)),
            dma((4, 2, 2)),
            dma((2,)),
            dma((2,)),
            dma((2, n)),
            dma((2, n)),
            dma((2, 3)),
            dma((2, 3)),
            dma((2 * n - 1,)),
            dma((2 * n - 1,)),
        ],
        compiler_params=pltpu.CompilerParams(
            collective_id=0, has_side_effects=True, vmem_limit_bytes=56 * 2**20
        ),
        cost_estimate=pl.CostEstimate(flops=6 * 10**9, bytes_accessed=12 * 2**20, transcendentals=0),
    )(receptor[0], channel_weight, owners, rotations, own, forward, inverse, lines, back_lines, fold)
    scores, best, best_all = pl.pallas_call(
        write_kernel,
        out_shape=(
            jax.ShapeDtypeStruct((2, 2, G, CELLS), BF16),
            jax.ShapeDtypeStruct((1, 1, 2, 2), F32),
            jax.ShapeDtypeStruct((1, 2, 2), F32),
        ),
        in_specs=[hbm, hbm],
        out_specs=(hbm, hbm, hbm),
        scratch_shapes=[
            pltpu.VMEM((2, 2, G, CELLS), BF16),
            pltpu.VMEM((2, 8, LANES), F32),
            pltpu.VMEM((1, 1, 2, 2), F32),
            pltpu.VMEM((1, 2, 2), F32),
            dma((3,)),
            dma((4,)),
        ],
        cost_estimate=pl.CostEstimate(flops=0, bytes_accessed=2**19, transcendentals=0),
    )(scores, tops)
    return scores[None, None], best, best_all


def solution(mesh):
    in_specs = (
        P("rec", None, "lig", None),
        P("lig", "rec", None, None, None, None),
        P(),
        P("lig", None),
        P("lig", None, None),
    )
    out_specs = (
        P("rec", "lig", None, None, None, None),
        P("rec", "lig", None, None),
        P("lig", None, None),
    )
    body = functools.partial(on_device, n=mesh.shape["rec"] // 2, ligs=mesh.shape["lig"])
    return jax.shard_map(body, mesh=mesh, in_specs=in_specs, out_specs=out_specs, check_vma=False)
```

```python
import functools

import jax
import jax.numpy as jnp
import ml_dtypes
import numpy as np
from jax import lax
from jax.experimental import pallas as pl
from jax.experimental.pallas import tpu as pltpu
from jax.sharding import PartitionSpec as P

MESH = pl.DeviceIdType.MESH
G = 32
CELLS = G * G
LANES = 128
FREQS = CELLS // 2
WIDE = FREQS // 2
BLOCKS = 2
PACKED = slice(WIDE - LANES, WIDE)
BF16 = jnp.bfloat16
F32 = jnp.float32


def split_table(table):
    high = table.astype(np.float32).astype(ml_dtypes.bfloat16)
    low = (table - high.astype(np.float64)).astype(np.float32).astype(ml_dtypes.bfloat16)
    return np.stack([high, low], 0)


def plane_frequencies():
    middle = G // 2
    lists = []
    for odd in range(2):
        pairs = [(ky, kz) for kz in range(1, middle) for ky in range(odd, G, 2)]
        pairs += [(ky, kz) for kz in (0, middle) for ky in range(odd, middle, 2) if ky]
        lists.append(pairs)
    first = lists[0] + [(0, 0), (0, middle)] + lists[1]
    second = lists[0] + [(middle, 0), (middle, middle)] + lists[1]
    return np.array(first), np.array(second)


def plane_tables():
    first, second = plane_frequencies()
    cell = np.arange(CELLS)
    y, z = cell // G, cell % G

    def angle(pairs):
        return 2.0 * np.pi * ((y[:, None] * pairs[:, 0] + z[:, None] * pairs[:, 1]) % G) / G

    paired = np.any(first != second, axis=1)
    real = np.cos(angle(first))
    imag = np.where(paired, np.cos(angle(second)), -np.sin(angle(first)))
    table = np.stack([real.reshape(CELLS, BLOCKS, WIDE), imag.reshape(CELLS, BLOCKS, WIDE)], 2)
    forward = table.transpose(1, 0, 2, 3).reshape(BLOCKS, CELLS, 2 * WIDE)
    inverse = forward[:, : CELLS // 2].transpose(0, 2, 1)
    weight = np.where(paired, 1.0, 2.0)
    return split_table(forward), split_table(inverse), weight.astype(np.float32).reshape(1, FREQS)


def mirror_table():
    row = np.arange(256)
    source = row // G * G + (G - row % G) % G
    table = np.zeros((256, 256))
    table[row, source] = np.where(row < 128, 1.0, -1.0)
    return table.astype(ml_dtypes.bfloat16)


def line_table(rows_in, rows_out, sign):
    group_in, x = rows_in
    group_out, k = rows_out
    angle = 2.0 * np.pi * ((k[:, None] * x[None, :]) % G) / G
    same = group_out[:, None] == group_in[None, :]
    cosine = np.where(same, np.cos(angle), 0.0)
    sine = np.where(same, np.sin(angle), 0.0) * sign
    return split_table(np.block([[cosine, sine], [-sine, cosine]]))


def line_tables():
    row = np.arange(128)
    plain = (row // G, row % G)
    rec = ((row // 2) % 4, (row // 8) * 2 + row % 2)
    pair = (plain[0][:64], plain[1][:64])
    forward = np.stack([line_table(plain, plain, 1.0), line_table(rec, plain, 1.0)], 0)
    return forward, line_table(pair, pair, -1.0)


def dot(a, b):
    return jnp.dot(a, b, preferred_element_type=F32)


def split(value):
    high = value.astype(BF16)
    return high, (value - high.astype(F32)).astype(BF16)


def line_transform(table, high, low):
    return dot(table[0], high) + dot(table[0], low) + dot(table[1], high)


def half_plane(data, forward, block, half):
    rows = pl.ds(pl.multiple_of(half * COLS, COLS), COLS)
    return dot(data, forward[0, block, rows]) + dot(data, forward[1, block, rows])


NEAR = (-2, -1, 1, 2)
FAR = (-5, 5)
COLS = CELLS // 2


def kernel(
    n,
    scale,
    rec_hbm,
    weight_hbm,
    owners_hbm,
    rotations_hbm,
    own_hbm,
    forward_hbm,
    inverse_hbm,
    lines_hbm,
    back_hbm,
    mirror_hbm,
    fold_hbm,
    scores_ref,
    tops_ref,
    rec_ref,
    weight_ref,
    owners_ref,
    rotations_ref,
    own,
    forward,
    inverse,
    lines,
    back_lines,
    mirror,
    fold,
    leaves,
    ends,
    partial,
    roots,
    gathered,
    rec_all,
    sums,
    stage,
    rec_stage,
    rec_spec,
    rec_cross,
    lig_spec,
    lig_cross,
    product,
    back,
    total,
    score_v,
    tops,
    small_sem,
    table_sem,
    out_sem,
    leaf_send,
    leaf_recv,
    end_send,
    end_recv,
    root_send,
    root_recv,
    first_send,
    first_recv,
    relay_send,
    relay_recv,
    last_send,
    last_recv,
    cross_send,
    cross_recv,
    rec_send,
    rec_recv,
    top_send,
    top_recv,
):
    rec = lax.axis_index("rec")
    lig = lax.axis_index("lig")
    side = rec // n
    me = lax.rem(rec, n)
    partner = lax.rem(rec + n, 2 * n)

    def shift(step):
        return lax.rem(me + n + step, n)

    def at(step):
        return side * n + shift(step)

    def over(step):
        return (1 - side) * n + shift(step)

    quad = lig // 4
    quad_peers = [quad * 4 + lax.rem(lig + step, 4) for step in range(1, 4)]
    line_peers = [lax.rem(lig + 4 * step, 16) for step in range(1, 4)]

    barrier = pltpu.get_barrier_semaphore()
    rec_peers = [over(step) for step in (-2, 2)] + [at(step) for step in (-3, 3, -2, 2, -1, 1)] + [over(0)]
    for peer in rec_peers:
        pl.semaphore_signal(barrier, inc=1, device_id={"rec": peer}, device_id_type=MESH)
    for peer in quad_peers + line_peers:
        pl.semaphore_signal(barrier, inc=1, device_id={"lig": peer}, device_id_type=MESH)

    small = [
        pltpu.make_async_copy(src, dst, small_sem.at[i])
        for i, (src, dst) in enumerate(
            [(rec_hbm, rec_ref), (owners_hbm, owners_ref), (rotations_hbm, rotations_ref), (weight_hbm, weight_ref)]
        )
    ]
    small[0].start()
    loads = [
        pltpu.make_async_copy(src, dst, table_sem.at[i])
        for i, (src, dst) in enumerate(
            [(own_hbm, own), (forward_hbm, forward), (lines_hbm, lines), (fold_hbm, fold), (inverse_hbm, inverse), (back_hbm, back_lines), (mirror_hbm, mirror)]
        )
    ]
    loads[0].start()
    for copy in small[1:] + loads[1:]:
        copy.start()
    small[0].wait()

    slab = jnp.concatenate([rec_ref[c].astype(F32) for c in range(4)], 0)
    rec_all[lig] = jnp.concatenate([slab[:, :COLS], slab[:, COLS:]], 0).astype(BF16)
    for copy in [loads[0]] + small[1:]:
        copy.wait()
    pl.semaphore_wait(barrier, len(rec_peers) + 6)

    sent = []

    def send(src, dst, send_sem, recv_sem, **where):
        copy = pltpu.make_async_remote_copy(
            src_ref=src,
            dst_ref=dst,
            send_sem=send_sem,
            recv_sem=recv_sem,
            device_id=where,
            device_id_type=MESH,
        )
        copy.start()
        sent.append(copy)
        return copy

    owner = [owners_ref[0, k] for k in range(2)]
    owner_z = [lax.rem(owner[k], n) for k in range(2)]
    owner_side = [owner[k] // n for k in range(2)]

    far = shift(n // 2)
    end = [
        send(own.at[far, :, :COLS], ends.at[0], end_send.at[0], end_recv.at[0], rec=at(-3)),
        send(own.at[far, :, COLS:], ends.at[1], end_send.at[1], end_recv.at[1], rec=at(3)),
    ]
    leaf = {}
    for j, step in ((1, -5), (2, 5), (0, 0)):
        for i, to in enumerate(NEAR):
            leaf[i, j] = send(
                own.at[shift(to + step)], leaves.at[i, j], leaf_send.at[i, j], leaf_recv.at[i, j], rec=at(to)
            )
    slabs = [
        send(rec_all.at[lig], rec_all.at[lig], rec_send.at[0, i], rec_recv.at[0, i], lig=peer)
        for i, peer in enumerate(quad_peers)
    ]
    for copy in slabs:
        copy.wait_recv()
    block = rec_all.at[pl.ds(quad * 4, 4)]
    slabs = [
        send(block, block, rec_send.at[1, i], rec_recv.at[1, i], lig=peer) for i, peer in enumerate(line_peers)
    ]

    for copy in end:
        copy.wait_recv()
    root = {}
    for j, step in ((1, -5), (2, 5), (0, 0)):
        shard = shift(step)
        for i in range(len(NEAR)):
            leaf[i, j].wait_recv()
        for k in range(2):
            away = lax.rem(owner_z[k] - me + n, n)
            value = own[shard]
            for i, to in enumerate(NEAR):
                value = jnp.where(away == (n - to) % n, leaves[i, j], value)
            parts = [value[:, :COLS], value[:, COLS:]]
            if j == 1:
                parts[0] = jnp.where(away == 3, ends[0], parts[0])
            if j == 2:
                parts[1] = jnp.where(away == n - 3, ends[1], parts[1])
            for half in range(2):
                partial[j, half, k] = parts[half]
            if j:
                for half in range(2):
                    slot = (j - 1) * 2 + side
                    root[j, half, k] = send(
                        partial.at[j, half, k],
                        roots.at[slot, k],
                        root_send.at[j - 1, half, k],
                        root_recv.at[slot, k],
                        rec=half * n + shard,
                    )
            else:
                root[0, k] = send(
                    partial.at[0, 1 - side, k],
                    roots.at[4, k],
                    root_send.at[2, 0, k],
                    root_recv.at[4, k],
                    rec=partner,
                )

    for copy in slabs:
        copy.wait_recv()
    loads[1].wait()
    loads[2].wait()
    loads[3].wait()
    grid = rec_all[...].astype(F32)
    rows = [grid[:, half * 8 : half * 8 + 8].reshape(128, COLS).astype(BF16) for half in range(2)]
    loads[6].wait()
    for block in range(BLOCKS):
        lanes = pl.ds(block * WIDE, WIDE)
        value = half_plane(rows[0], forward, block, 0) + half_plane(rows[1], forward, block, 1)
        for part in range(2):
            high, low = split(value[:, part * WIDE : (part + 1) * WIDE])
            rec_stage[0, part * 128 : (part + 1) * 128, lanes] = high
            rec_stage[1, part * 128 : (part + 1) * 128, lanes] = low
    value = line_transform(lines.at[1], rec_stage[0], rec_stage[1]) * fold[...]
    for c in range(4):
        for part in range(2):
            at_row = slice(part * 128 + c * 32, part * 128 + c * 32 + 32)
            rec_spec[at_row] = value[at_row] * weight_ref[c]
    value = rec_spec[:, PACKED]
    high, low = split(value)
    turned = dot(mirror[...], high) + dot(mirror[...], low)
    a, b, c, d = value[:128], value[128:], turned[:128], turned[128:]
    pair = lax.broadcasted_iota(jnp.int32, (128, LANES), 1) >= LANES - 2
    rec_spec[:128, PACKED] = jnp.where(pair, (a + b + c - d) * 0.25, a)
    rec_spec[128:, PACKED] = jnp.where(pair, (b - a + c + d) * 0.25, b)
    rec_cross[:128] = jnp.where(pair, (a - b + c + d) * 0.25, 0.0)
    rec_cross[128:] = jnp.where(pair, (a + b + d - c) * 0.25, 0.0)

    def root_wait(slot, k):
        pltpu.make_async_copy(roots.at[slot, k], roots.at[slot, k], root_recv.at[slot, k]).wait()

    first, relay, last = {}, {}, {}
    cross = [[], []]

    def spread(k, shard):
        ref = gathered.at[k, shard, side]
        slot = len(cross[k])
        cross[k].append(send(ref, ref, cross_send.at[k, slot], cross_recv.at[k, slot], rec=partner))

    def gather_first(k):
        for slot in range(5):
            root_wait(slot, k)
        away = lax.rem(owner_z[k] - me + n, n)
        below = jnp.logical_or(away > n // 2, jnp.logical_and(away == n // 2, side == 1))
        inner = jnp.logical_or(away <= 2, away >= n - 2)
        here = owner_side[k] == side
        middle = jnp.where(here, partial[0, side, k], roots[4, k])
        up = jnp.where(owner_side[k] == 0, roots[0, k], roots[1, k])
        down = jnp.where(owner_side[k] == 0, roots[2, k], roots[3, k])
        gathered[k, me, side] = jnp.where(inner, middle, jnp.where(below, down, up))
        mine = gathered.at[k, me, side]
        for i, to in enumerate(FAR + NEAR):
            first[k, to] = send(mine, mine, first_send.at[i, k], first_recv.at[i, k], rec=at(to))
        spread(k, me)

    def gather_relay(k):
        for j, to in enumerate(FAR):
            first[k, to].wait_recv()
            shard = shift(-to)
            ref = gathered.at[k, shard, side]
            for i, near in enumerate(NEAR):
                relay[i, j, k] = send(ref, ref, relay_send.at[i, j, k], relay_recv.at[i, j, k], rec=at(near))
            if j == k:
                last[k] = send(ref, ref, last_send.at[k], last_recv.at[k], rec=at(-3 if to < 0 else 3))
            spread(k, shard)
        for to in NEAR:
            first[k, to].wait_recv()
            spread(k, shift(-to))

    def gather_cross(k):
        for j, to in enumerate(FAR):
            for i, near in enumerate(NEAR):
                relay[i, j, k].wait_recv()
                spread(k, shift(-near - to))
        last[k].wait_recv()
        spread(k, far)

    for k in range(2):
        gather_first(k)
    for k in range(2):
        gather_relay(k)
    def half_rows(k, half):
        return gathered[k, :, half].reshape(256, COLS)

    for k in range(2):
        gather_cross(k)
        data = half_rows(k, side)
        for block in range(BLOCKS):
            sums[k, block] = half_plane(data, forward, block, side)

    sub = lax.broadcasted_iota(jnp.int32, (8, LANES), 0)
    lane = lax.broadcasted_iota(jnp.int32, (8, LANES), 1)
    top = jnp.zeros((8, LANES), F32)
    for k in range(2):
        for copy in cross[k]:
            copy.wait_recv()

        data = half_rows(k, 1 - side)
        for block in range(BLOCKS):
            lanes = pl.ds(block * WIDE, WIDE)
            value = sums[k, block] + half_plane(data, forward, block, 1 - side)
            for part in range(2):
                high, low = split(value[:, part * WIDE : (part + 1) * WIDE])
                for grid in range(2):
                    stage[grid, 0, part * 128 : (part + 1) * 128, lanes] = high[grid * 128 : grid * 128 + 128]
                    stage[grid, 1, part * 128 : (part + 1) * 128, lanes] = low[grid * 128 : grid * 128 + 128]

        for grid in range(2):
            value = line_transform(lines.at[0], stage[grid, 0], stage[grid, 1]).astype(BF16)
            lig_spec[...] = value.astype(F32)
            lig_cross[...] = dot(mirror[...], value[:, PACKED])
            real = imag = 0.0
            real_cross = imag_cross = 0.0
            for c in range(4):
                re, im = slice(c * 32, c * 32 + 32), slice(128 + c * 32, 128 + c * 32 + 32)
                real += rec_spec[re] * lig_spec[re] + rec_spec[im] * lig_spec[im]
                imag += rec_spec[re] * lig_spec[im] - rec_spec[im] * lig_spec[re]
                real_cross += rec_cross[re] * lig_cross[re] + rec_cross[im] * lig_cross[im]
                imag_cross += rec_cross[re] * lig_cross[im] - rec_cross[im] * lig_cross[re]
            for part, whole, crossed in ((0, real, real_cross), (64, imag, imag_cross)):
                at_row = slice(part + grid * 32, part + grid * 32 + 32)
                product[at_row] = whole
                product[at_row, PACKED] = whole[:, PACKED] + crossed

        if k == 0:
            loads[4].wait()
            loads[5].wait()
        high, low = split(product[...])
        back[...] = line_transform(back_lines, high, low)
        folded = []
        for block in range(BLOCKS):
            lanes = slice(block * WIDE, (block + 1) * WIDE)
            high, low = split(jnp.concatenate([back[:64, lanes], back[64:, lanes]], 1))
            part = dot(jnp.concatenate([high, low], 0), inverse[0, block])
            folded.append(part[:64] + part[64:] + dot(high, inverse[1, block]))
        total[:, : CELLS // 2] = folded[0] + folded[1]
        total[:, CELLS // 2 :] = folded[0] - folded[1]

        pair = [total[:32] * scale, total[32:] * scale]
        for j in range(2):
            value = jnp.where(rotations_ref[0, k, j] == 0, pair[0], pair[1])
            score_v[k, j] = value.astype(BF16)
            top = jnp.where(jnp.logical_and(sub == k, lane == j), jnp.max(value), top)

    earlier = list(sent)
    tops[0] = top
    steps = sorted(range(1, n), key=lambda step: -min(step, n - step))
    peers = [over(step) for step in steps[:7]] + [at(step) for step in steps[:7]]
    peers += [over(step) for step in steps[7:]] + [at(step) for step in steps[7:]] + [over(0)]
    copies = [
        send(tops.at[0], tops.at[1 + i], top_send.at[i], top_recv.at[i], rec=peer) for i, peer in enumerate(peers)
    ]
    out = pltpu.make_async_copy(score_v, scores_ref, out_sem)
    out.start()
    tops_ref[0] = top
    for copy in earlier:
        copy.wait_send()
    out.wait()
    for copy in copies:
        copy.wait_recv()
    tops_ref[1] = jnp.max(tops[...], axis=0)
    for copy in copies:
        copy.wait_send()


def write_kernel(scores_in, tops_in, scores_ref, best_ref, best_all_ref, held, tops, best, best_all, in_sem, out_sem):
    reads = [pltpu.make_async_copy(tops_in, tops, in_sem.at[2])]
    reads += [pltpu.make_async_copy(scores_in.at[k], held.at[k], in_sem.at[k]) for k in range(2)]
    writes = [pltpu.make_async_copy(held.at[k], scores_ref.at[k], out_sem.at[k]) for k in range(2)]
    writes.append(pltpu.make_async_copy(best, best_ref, out_sem.at[2]))
    writes.append(pltpu.make_async_copy(best_all, best_all_ref, out_sem.at[3]))
    for copy in reads:
        copy.start()
    reads[0].wait()
    best[0, 0] = tops[0, :2, :2]
    best_all[0] = tops[1, :2, :2]
    for copy in writes[2:]:
        copy.start()
    for k in range(2):
        reads[1 + k].wait()
        writes[k].start()
    for copy in writes:
        copy.wait()


def on_device(receptor, ligand_pool, channel_weight, owners, rotations, n, ligs):
    channels = ligand_pool.shape[3]
    scale = 1.0 / (float(G) ** 3 * float(channels * G**3) ** 0.5)
    forward, inverse, fold = plane_tables()
    lines, back_lines = line_tables()
    mirror = mirror_table()
    own = ligand_pool.reshape(n, 16, CELLS)
    vmem = pl.BlockSpec(memory_space=pltpu.VMEM)
    hbm = pl.BlockSpec(memory_space=pl.ANY)
    dma = pltpu.SemaphoreType.DMA
    scores, tops = pl.pallas_call(
        functools.partial(kernel, n, scale),
        out_shape=(
            jax.ShapeDtypeStruct((2, 2, G, CELLS), BF16),
            jax.ShapeDtypeStruct((2, 8, LANES), F32),
        ),
        in_specs=[hbm] * 11,
        out_specs=(hbm, vmem),
        scratch_shapes=[
            pltpu.VMEM((channels, 2, CELLS), BF16),
            pltpu.SMEM((channels,), F32),
            pltpu.SMEM(owners.shape, jnp.int32),
            pltpu.SMEM(rotations.shape, jnp.int32),
            pltpu.VMEM((n, 16, CELLS), BF16),
            pltpu.VMEM(forward.shape, BF16),
            pltpu.VMEM(inverse.shape, BF16),
            pltpu.VMEM(lines.shape, BF16),
            pltpu.VMEM(back_lines.shape, BF16),
            pltpu.VMEM(mirror.shape, BF16),
            pltpu.VMEM(fold.shape, F32),
            pltpu.VMEM((4, 3, 16, CELLS), BF16),
            pltpu.VMEM((2, 16, COLS), BF16),
            pltpu.VMEM((3, 2, 2, 16, COLS), BF16),
            pltpu.VMEM((5, 2, 16, COLS), BF16),
            pltpu.VMEM((2, n, 2, 16, COLS), BF16),
            pltpu.VMEM((ligs, 16, COLS), BF16),
            pltpu.VMEM((2, BLOCKS, 256, 2 * WIDE), F32),
            pltpu.VMEM((2, 2, 256, FREQS), BF16),
            pltpu.VMEM((2, 256, FREQS), BF16),
            pltpu.VMEM((256, FREQS), F32),
            pltpu.VMEM((256, LANES), F32),
            pltpu.VMEM((256, FREQS), F32),
            pltpu.VMEM((256, LANES), F32),
            pltpu.VMEM((128, FREQS), F32),
            pltpu.VMEM((128, FREQS), F32),
            pltpu.VMEM((64, CELLS), F32),
            pltpu.VMEM((2, 2, G, CELLS), BF16),
            pltpu.VMEM((2 * n, 8, LANES), F32),
            dma((4,)),
            dma((7,)),
            dma,
            dma((4, 3)),
            dma((4, 3)),
            dma((2,)),
            dma((2,)),
            dma((3, 2, 2)),
            dma((5, 2)),
            dma((6, 2)),
            dma((6, 2)),
            dma((4, 2, 2)),
            dma((4, 2, 2)),
            dma((2,)),
            dma((2,)),
            dma((2, n)),
            dma((2, n)),
            dma((2, 3)),
            dma((2, 3)),
            dma((2 * n - 1,)),
            dma((2 * n - 1,)),
        ],
        compiler_params=pltpu.CompilerParams(
            collective_id=0, has_side_effects=True, vmem_limit_bytes=56 * 2**20
        ),
        cost_estimate=pl.CostEstimate(flops=6 * 10**9, bytes_accessed=12 * 2**20, transcendentals=0),
    )(receptor[0], channel_weight, owners, rotations, own, forward, inverse, lines, back_lines, mirror, fold)
    scores, best, best_all = pl.pallas_call(
        write_kernel,
        out_shape=(
            jax.ShapeDtypeStruct((2, 2, G, CELLS), BF16),
            jax.ShapeDtypeStruct((1, 1, 2, 2), F32),
            jax.ShapeDtypeStruct((1, 2, 2), F32),
        ),
        in_specs=[hbm, hbm],
        out_specs=(hbm, hbm, hbm),
        scratch_shapes=[
            pltpu.VMEM((2, 2, G, CELLS), BF16),
            pltpu.VMEM((2, 8, LANES), F32),
            pltpu.VMEM((1, 1, 2, 2), F32),
            pltpu.VMEM((1, 2, 2), F32),
            dma((3,)),
            dma((4,)),
        ],
        cost_estimate=pl.CostEstimate(flops=0, bytes_accessed=2**19, transcendentals=0),
    )(scores, tops)
    return scores[None, None], best, best_all


def solution(mesh):
    in_specs = (
        P("rec", None, "lig", None),
        P("lig", "rec", None, None, None, None),
        P(),
        P("lig", None),
        P("lig", None, None),
    )
    out_specs = (
        P("rec", "lig", None, None, None, None),
        P("rec", "lig", None, None),
        P("lig", None, None),
    )
    body = functools.partial(on_device, n=mesh.shape["rec"] // 2, ligs=mesh.shape["lig"])
    return jax.shard_map(body, mesh=mesh, in_specs=in_specs, out_specs=out_specs, check_vma=False)
```

```python
import functools

import jax
import jax.numpy as jnp
import ml_dtypes
import numpy as np
from jax import lax
from jax.experimental import pallas as pl
from jax.experimental.pallas import tpu as pltpu
from jax.sharding import PartitionSpec as P

MESH = pl.DeviceIdType.MESH
G = 32
CELLS = G * G
LANES = 128
FREQS = CELLS // 2
WIDE = FREQS // 2
BLOCKS = 2
PACKED = slice(WIDE - LANES, WIDE)
BF16 = jnp.bfloat16
F32 = jnp.float32


def split_table(table):
    high = table.astype(np.float32).astype(ml_dtypes.bfloat16)
    low = (table - high.astype(np.float64)).astype(np.float32).astype(ml_dtypes.bfloat16)
    return np.stack([high, low], 0)


def plane_frequencies():
    middle = G // 2
    lists = []
    for odd in range(2):
        pairs = [(ky, kz) for kz in range(1, middle) for ky in range(odd, G, 2)]
        pairs += [(ky, kz) for kz in (0, middle) for ky in range(odd, middle, 2) if ky]
        lists.append(pairs)
    first = lists[0] + [(0, 0), (0, middle)] + lists[1]
    second = lists[0] + [(middle, 0), (middle, middle)] + lists[1]
    return np.array(first), np.array(second)


def plane_tables():
    first, second = plane_frequencies()
    cell = np.arange(CELLS)
    y, z = cell // G, cell % G

    def angle(pairs):
        return 2.0 * np.pi * ((y[:, None] * pairs[:, 0] + z[:, None] * pairs[:, 1]) % G) / G

    paired = np.any(first != second, axis=1)
    real = np.cos(angle(first))
    imag = np.where(paired, np.cos(angle(second)), -np.sin(angle(first)))
    table = np.stack([real.reshape(CELLS, BLOCKS, WIDE), imag.reshape(CELLS, BLOCKS, WIDE)], 2)
    forward = table.transpose(1, 0, 2, 3).reshape(BLOCKS, CELLS, 2 * WIDE)
    inverse = forward[:, : CELLS // 2].transpose(0, 2, 1)
    weight = np.where(paired, 1.0, 2.0)
    return split_table(forward), split_table(inverse), weight.astype(np.float32).reshape(1, FREQS)


def mirror_table():
    row = np.arange(256)
    source = row // G * G + (G - row % G) % G
    table = np.zeros((256, 256))
    table[row, source] = np.where(row < 128, 1.0, -1.0)
    return table.astype(ml_dtypes.bfloat16)


def line_table(rows_in, rows_out, sign):
    group_in, x = rows_in
    group_out, k = rows_out
    angle = 2.0 * np.pi * ((k[:, None] * x[None, :]) % G) / G
    same = group_out[:, None] == group_in[None, :]
    cosine = np.where(same, np.cos(angle), 0.0)
    sine = np.where(same, np.sin(angle), 0.0) * sign
    return split_table(np.block([[cosine, sine], [-sine, cosine]]))


def line_tables():
    row = np.arange(128)
    plain = (row // G, row % G)
    rec = ((row // 2) % 4, (row // 8) * 2 + row % 2)
    pair = (plain[0][:64], plain[1][:64])
    forward = np.stack([line_table(plain, plain, 1.0), line_table(rec, plain, 1.0)], 0)
    return forward, line_table(pair, pair, -1.0)


def dot(a, b):
    return jnp.dot(a, b, preferred_element_type=F32)


def split(value):
    high = value.astype(BF16)
    return high, (value - high.astype(F32)).astype(BF16)


def line_transform(table, high, low):
    return dot(table[0], high) + dot(table[0], low) + dot(table[1], high)


def half_plane(data, forward, block, half):
    rows = pl.ds(pl.multiple_of(half * COLS, COLS), COLS)
    return dot(data, forward[0, block, rows]) + dot(data, forward[1, block, rows])


NEAR = (-2, -1, 1, 2)
FAR = (-5, 5)
COLS = CELLS // 2


def kernel(
    n,
    scale,
    rec_hbm,
    weight_hbm,
    owners_hbm,
    rotations_hbm,
    own_hbm,
    forward_hbm,
    inverse_hbm,
    lines_hbm,
    back_hbm,
    mirror_hbm,
    fold_hbm,
    scores_ref,
    tops_ref,
    rec_ref,
    weight_ref,
    owners_ref,
    rotations_ref,
    own,
    forward,
    inverse,
    lines,
    back_lines,
    mirror,
    fold,
    leaves,
    ends,
    partial,
    roots,
    gathered,
    rec_all,
    sums,
    stage,
    rec_stage,
    rec_spec,
    rec_cross,
    lig_spec,
    lig_cross,
    product,
    back,
    total,
    score_v,
    tops,
    known_sem,
    small_sem,
    table_sem,
    out_sem,
    leaf_send,
    leaf_recv,
    end_send,
    end_recv,
    root_send,
    root_recv,
    first_send,
    first_recv,
    relay_send,
    relay_recv,
    last_send,
    last_recv,
    cross_send,
    cross_recv,
    rec_send,
    rec_recv,
    top_send,
    top_recv,
):
    rec = lax.axis_index("rec")
    lig = lax.axis_index("lig")
    side = rec // n
    me = lax.rem(rec, n)
    partner = lax.rem(rec + n, 2 * n)

    def shift(step):
        return lax.rem(me + n + step, n)

    def at(step):
        return side * n + shift(step)

    def over(step):
        return (1 - side) * n + shift(step)

    quad = lig // 4
    quad_peers = [quad * 4 + lax.rem(lig + step, 4) for step in range(1, 4)]
    line_peers = [lax.rem(lig + 4 * step, 16) for step in range(1, 4)]

    barrier = pltpu.get_barrier_semaphore()
    rec_peers = [at(step) for step in (-3, 3, -2, 2)] + [over(0), at(-1), at(1)]
    for peer in rec_peers:
        pl.semaphore_signal(barrier, inc=1, device_id={"rec": peer}, device_id_type=MESH)
    for peer in quad_peers + line_peers:
        pl.semaphore_signal(barrier, inc=1, device_id={"lig": peer}, device_id_type=MESH)

    small = [
        pltpu.make_async_copy(src, dst, small_sem.at[i])
        for i, (src, dst) in enumerate(
            [(rec_hbm, rec_ref), (owners_hbm, owners_ref), (rotations_hbm, rotations_ref), (weight_hbm, weight_ref)]
        )
    ]
    small[0].start()
    loads = [
        pltpu.make_async_copy(src, dst, table_sem.at[i])
        for i, (src, dst) in enumerate(
            [(own_hbm, own), (forward_hbm, forward), (lines_hbm, lines), (fold_hbm, fold), (inverse_hbm, inverse), (back_hbm, back_lines), (mirror_hbm, mirror)]
        )
    ]
    loads[0].start()
    for copy in small[1:] + loads[1:]:
        copy.start()
    small[0].wait()

    slab = jnp.concatenate([rec_ref[c].astype(F32) for c in range(4)], 0)
    rec_all[lig] = jnp.concatenate([slab[:, :COLS], slab[:, COLS:]], 0).astype(BF16)
    for copy in [loads[0]] + small[1:]:
        copy.wait()
    pl.semaphore_wait(barrier, len(rec_peers) + 6)

    sent = []

    def send(src, dst, send_sem, recv_sem, **where):
        copy = pltpu.make_async_remote_copy(
            src_ref=src,
            dst_ref=dst,
            send_sem=send_sem,
            recv_sem=recv_sem,
            device_id=where,
            device_id_type=MESH,
        )
        copy.start()
        sent.append(copy)
        return copy

    owner = [owners_ref[0, k] for k in range(2)]
    owner_z = [lax.rem(owner[k], n) for k in range(2)]
    owner_side = [owner[k] // n for k in range(2)]

    far = shift(n // 2)
    end = [
        send(own.at[far, :, :COLS], ends.at[0], end_send.at[0], end_recv.at[0], rec=at(-3)),
        send(own.at[far, :, COLS:], ends.at[1], end_send.at[1], end_recv.at[1], rec=at(3)),
    ]
    leaf = {}
    for j, step in ((1, -5), (2, 5), (0, 0)):
        for i, to in enumerate(NEAR):
            leaf[i, j] = send(
                own.at[shift(to + step)], leaves.at[i, j], leaf_send.at[i, j], leaf_recv.at[i, j], rec=at(to)
            )
    slabs = [
        send(rec_all.at[lig], rec_all.at[lig], rec_send.at[0, i], rec_recv.at[0, i], lig=peer)
        for i, peer in enumerate(quad_peers)
    ]
    for copy in slabs:
        copy.wait_recv()
    block = rec_all.at[pl.ds(quad * 4, 4)]
    slabs = [
        send(block, block, rec_send.at[1, i], rec_recv.at[1, i], lig=peer) for i, peer in enumerate(line_peers)
    ]

    for copy in end:
        copy.wait_recv()
    for step in (-2, 2):
        pl.semaphore_signal(known_sem, inc=1, device_id={"rec": at(step)}, device_id_type=MESH)
    root = {}
    for j, step in ((1, -5), (2, 5), (0, 0)):
        shard = shift(step)
        for i in range(len(NEAR)):
            leaf[i, j].wait_recv()
        if j == 1:
            pl.semaphore_wait(known_sem, 2)
        for k in range(2):
            away = lax.rem(owner_z[k] - me + n, n)
            value = own[shard]
            for i, to in enumerate(NEAR):
                value = jnp.where(away == (n - to) % n, leaves[i, j], value)
            parts = [value[:, :COLS], value[:, COLS:]]
            if j == 1:
                parts[0] = jnp.where(away == 3, ends[0], parts[0])
            if j == 2:
                parts[1] = jnp.where(away == n - 3, ends[1], parts[1])
            for half in range(2):
                partial[j, half, k] = parts[half]
            if j:
                for half in range(2):
                    slot = (j - 1) * 2 + side
                    root[j, half, k] = send(
                        partial.at[j, half, k],
                        roots.at[slot, k],
                        root_send.at[j - 1, half, k],
                        root_recv.at[slot, k],
                        rec=half * n + shard,
                    )
            else:
                root[0, k] = send(
                    partial.at[0, 1 - side, k],
                    roots.at[4, k],
                    root_send.at[2, 0, k],
                    root_recv.at[4, k],
                    rec=partner,
                )

    for copy in slabs:
        copy.wait_recv()
    loads[1].wait()
    loads[2].wait()
    loads[3].wait()
    grid = rec_all[...].astype(F32)
    rows = [grid[:, half * 8 : half * 8 + 8].reshape(128, COLS).astype(BF16) for half in range(2)]
    loads[6].wait()
    for block in range(BLOCKS):
        lanes = pl.ds(block * WIDE, WIDE)
        value = half_plane(rows[0], forward, block, 0) + half_plane(rows[1], forward, block, 1)
        for part in range(2):
            high, low = split(value[:, part * WIDE : (part + 1) * WIDE])
            rec_stage[0, part * 128 : (part + 1) * 128, lanes] = high
            rec_stage[1, part * 128 : (part + 1) * 128, lanes] = low
    value = line_transform(lines.at[1], rec_stage[0], rec_stage[1]) * fold[...]
    for c in range(4):
        for part in range(2):
            at_row = slice(part * 128 + c * 32, part * 128 + c * 32 + 32)
            rec_spec[at_row] = value[at_row] * weight_ref[c]
    value = rec_spec[:, PACKED]
    high, low = split(value)
    turned = dot(mirror[...], high) + dot(mirror[...], low)
    a, b, c, d = value[:128], value[128:], turned[:128], turned[128:]
    pair = lax.broadcasted_iota(jnp.int32, (128, LANES), 1) >= LANES - 2
    rec_spec[:128, PACKED] = jnp.where(pair, (a + b + c - d) * 0.25, a)
    rec_spec[128:, PACKED] = jnp.where(pair, (b - a + c + d) * 0.25, b)
    rec_cross[:128] = jnp.where(pair, (a - b + c + d) * 0.25, 0.0)
    rec_cross[128:] = jnp.where(pair, (a + b + d - c) * 0.25, 0.0)

    def root_wait(slot, k):
        pltpu.make_async_copy(roots.at[slot, k], roots.at[slot, k], root_recv.at[slot, k]).wait()

    first, relay, last = {}, {}, {}
    cross = [[], []]

    def spread(k, lo, hi):
        slot = len(cross[k])
        cross[k].append(
            send(
                gathered.at[k, 0, lo:hi],
                gathered.at[k, 1, lo:hi],
                cross_send.at[k, slot],
                cross_recv.at[k, slot],
                rec=partner,
            )
        )

    def gather_first(k):
        for slot in range(5):
            root_wait(slot, k)
        away = lax.rem(owner_z[k] - me + n, n)
        below = jnp.logical_or(away > n // 2, jnp.logical_and(away == n // 2, side == 1))
        inner = jnp.logical_or(away <= 2, away >= n - 2)
        here = owner_side[k] == side
        middle = jnp.where(here, partial[0, side, k], roots[4, k])
        up = jnp.where(owner_side[k] == 0, roots[0, k], roots[1, k])
        down = jnp.where(owner_side[k] == 0, roots[2, k], roots[3, k])
        gathered[k, 0, 8] = jnp.where(inner, middle, jnp.where(below, down, up))
        for i, to in enumerate(FAR + NEAR):
            first[k, to] = send(
                gathered.at[k, 0, 8],
                gathered.at[k, 0, 8 - to],
                first_send.at[i, k],
                first_recv.at[i, k],
                rec=at(to),
            )

    def gather_relay(k):
        for j, to in enumerate(FAR):
            first[k, to].wait_recv()
            ref = gathered.at[k, 0, 8 - to]
            for i, near in enumerate(NEAR):
                relay[i, j, k] = send(
                    ref, gathered.at[k, 0, 8 - to - near], relay_send.at[i, j, k], relay_recv.at[i, j, k], rec=at(near)
                )
            if j == k:
                last[k] = send(
                    ref, gathered.at[k, 0, 0], last_send.at[k], last_recv.at[k], rec=at(-3 if to < 0 else 3)
                )
            spread(k, 8 - to, 9 - to)
        for to in NEAR:
            first[k, to].wait_recv()
        spread(k, 6, 11)

    def gather_cross(k):
        for j, to in enumerate(FAR):
            for pair in ((0, 1), (2, 3)):
                for i in pair:
                    relay[i, j, k].wait_recv()
                lo = 8 - to - max(NEAR[i] for i in pair)
                spread(k, lo, lo + 2)
        last[k].wait_recv()
        spread(k, 0, 1)

    for k in range(2):
        gather_first(k)
    for k in range(2):
        gather_relay(k)
    def half_rows(k, line):
        return jnp.concatenate([gathered[k, line, lax.rem(s + n + 8 - me, n)] for s in range(n)], 0)

    for k in range(2):
        gather_cross(k)
        data = half_rows(k, 0)
        for block in range(BLOCKS):
            sums[k, block] = half_plane(data, forward, block, side)

    sub = lax.broadcasted_iota(jnp.int32, (8, LANES), 0)
    lane = lax.broadcasted_iota(jnp.int32, (8, LANES), 1)
    top = jnp.zeros((8, LANES), F32)
    for k in range(2):
        for copy in cross[k]:
            copy.wait_recv()

        data = half_rows(k, 1)
        for block in range(BLOCKS):
            lanes = pl.ds(block * WIDE, WIDE)
            value = sums[k, block] + half_plane(data, forward, block, 1 - side)
            for part in range(2):
                high, low = split(value[:, part * WIDE : (part + 1) * WIDE])
                for grid in range(2):
                    stage[grid, 0, part * 128 : (part + 1) * 128, lanes] = high[grid * 128 : grid * 128 + 128]
                    stage[grid, 1, part * 128 : (part + 1) * 128, lanes] = low[grid * 128 : grid * 128 + 128]

        for grid in range(2):
            value = line_transform(lines.at[0], stage[grid, 0], stage[grid, 1]).astype(BF16)
            lig_spec[...] = value.astype(F32)
            lig_cross[...] = dot(mirror[...], value[:, PACKED])
            real = imag = 0.0
            real_cross = imag_cross = 0.0
            for c in range(4):
                re, im = slice(c * 32, c * 32 + 32), slice(128 + c * 32, 128 + c * 32 + 32)
                real += rec_spec[re] * lig_spec[re] + rec_spec[im] * lig_spec[im]
                imag += rec_spec[re] * lig_spec[im] - rec_spec[im] * lig_spec[re]
                real_cross += rec_cross[re] * lig_cross[re] + rec_cross[im] * lig_cross[im]
                imag_cross += rec_cross[re] * lig_cross[im] - rec_cross[im] * lig_cross[re]
            for part, whole, crossed in ((0, real, real_cross), (64, imag, imag_cross)):
                at_row = slice(part + grid * 32, part + grid * 32 + 32)
                product[at_row] = whole
                product[at_row, PACKED] = whole[:, PACKED] + crossed

        if k == 0:
            loads[4].wait()
            loads[5].wait()
        high, low = split(product[...])
        back[...] = line_transform(back_lines, high, low)
        folded = []
        for block in range(BLOCKS):
            lanes = slice(block * WIDE, (block + 1) * WIDE)
            high, low = split(jnp.concatenate([back[:64, lanes], back[64:, lanes]], 1))
            part = dot(jnp.concatenate([high, low], 0), inverse[0, block])
            folded.append(part[:64] + part[64:] + dot(high, inverse[1, block]))
        total[:, : CELLS // 2] = folded[0] + folded[1]
        total[:, CELLS // 2 :] = folded[0] - folded[1]

        def store_scores(k):
            for j in range(2):
                value = jnp.where(rotations_ref[0, k, j] == 0, total[:32], total[32:])
                score_v[k, j] = (value * scale).astype(BF16)

        tall = [jnp.max(total[:32]) * scale, jnp.max(total[32:]) * scale]
        for j in range(2):
            value = jnp.where(rotations_ref[0, k, j] == 0, tall[0], tall[1])
            top = jnp.where(jnp.logical_and(sub == k, lane == j), value, top)
        if k == 0:
            store_scores(0)

    earlier = list(sent)
    tops[0] = top
    two = pl.ds(0, 2)
    steps = sorted(range(1, n), key=lambda step: -min(step, n - step))
    peers = [over(step) for step in steps[:7]] + [at(step) for step in steps[:7]]
    peers += [over(step) for step in steps[7:]] + [at(step) for step in steps[7:]] + [over(0)]
    copies = [
        send(tops.at[0, two], tops.at[1 + i, two], top_send.at[i], top_recv.at[i], rec=peer)
        for i, peer in enumerate(peers)
    ]
    store_scores(1)
    out = pltpu.make_async_copy(score_v, scores_ref, out_sem)
    out.start()
    tops_ref[0] = top
    for copy in earlier:
        copy.wait_send()
    out.wait()
    for copy in copies:
        copy.wait_recv()
    tops_ref[1, :2] = jnp.max(tops[:, :2], axis=0)
    for copy in copies:
        copy.wait_send()


def write_kernel(scores_in, tops_in, scores_ref, best_ref, best_all_ref, held, tops, best, best_all, in_sem, out_sem):
    reads = [pltpu.make_async_copy(tops_in, tops, in_sem.at[2])]
    reads += [pltpu.make_async_copy(scores_in.at[k], held.at[k], in_sem.at[k]) for k in range(2)]
    writes = [pltpu.make_async_copy(held.at[k], scores_ref.at[k], out_sem.at[k]) for k in range(2)]
    writes.append(pltpu.make_async_copy(best, best_ref, out_sem.at[2]))
    writes.append(pltpu.make_async_copy(best_all, best_all_ref, out_sem.at[3]))
    for copy in reads:
        copy.start()
    reads[0].wait()
    best[0, 0] = tops[0, :2, :2]
    best_all[0] = tops[1, :2, :2]
    for copy in writes[2:]:
        copy.start()
    for k in range(2):
        reads[1 + k].wait()
        writes[k].start()
    for copy in writes:
        copy.wait()


def on_device(receptor, ligand_pool, channel_weight, owners, rotations, n, ligs):
    channels = ligand_pool.shape[3]
    scale = 1.0 / (float(G) ** 3 * float(channels * G**3) ** 0.5)
    forward, inverse, fold = plane_tables()
    lines, back_lines = line_tables()
    mirror = mirror_table()
    own = ligand_pool.reshape(n, 16, CELLS)
    vmem = pl.BlockSpec(memory_space=pltpu.VMEM)
    hbm = pl.BlockSpec(memory_space=pl.ANY)
    dma = pltpu.SemaphoreType.DMA
    scores, tops = pl.pallas_call(
        functools.partial(kernel, n, scale),
        out_shape=(
            jax.ShapeDtypeStruct((2, 2, G, CELLS), BF16),
            jax.ShapeDtypeStruct((2, 8, LANES), F32),
        ),
        in_specs=[hbm] * 11,
        out_specs=(hbm, vmem),
        scratch_shapes=[
            pltpu.VMEM((channels, 2, CELLS), BF16),
            pltpu.SMEM((channels,), F32),
            pltpu.SMEM(owners.shape, jnp.int32),
            pltpu.SMEM(rotations.shape, jnp.int32),
            pltpu.VMEM((n, 16, CELLS), BF16),
            pltpu.VMEM(forward.shape, BF16),
            pltpu.VMEM(inverse.shape, BF16),
            pltpu.VMEM(lines.shape, BF16),
            pltpu.VMEM(back_lines.shape, BF16),
            pltpu.VMEM(mirror.shape, BF16),
            pltpu.VMEM(fold.shape, F32),
            pltpu.VMEM((4, 3, 16, CELLS), BF16),
            pltpu.VMEM((2, 16, COLS), BF16),
            pltpu.VMEM((3, 2, 2, 16, COLS), BF16),
            pltpu.VMEM((5, 2, 16, COLS), BF16),
            pltpu.VMEM((2, 2, n, 16, COLS), BF16),
            pltpu.VMEM((ligs, 16, COLS), BF16),
            pltpu.VMEM((2, BLOCKS, 256, 2 * WIDE), F32),
            pltpu.VMEM((2, 2, 256, FREQS), BF16),
            pltpu.VMEM((2, 256, FREQS), BF16),
            pltpu.VMEM((256, FREQS), F32),
            pltpu.VMEM((256, LANES), F32),
            pltpu.VMEM((256, FREQS), F32),
            pltpu.VMEM((256, LANES), F32),
            pltpu.VMEM((128, FREQS), F32),
            pltpu.VMEM((128, FREQS), F32),
            pltpu.VMEM((64, CELLS), F32),
            pltpu.VMEM((2, 2, G, CELLS), BF16),
            pltpu.VMEM((2 * n, 8, LANES), F32),
            pltpu.SemaphoreType.REGULAR,
            dma((4,)),
            dma((7,)),
            dma,
            dma((4, 3)),
            dma((4, 3)),
            dma((2,)),
            dma((2,)),
            dma((3, 2, 2)),
            dma((5, 2)),
            dma((6, 2)),
            dma((6, 2)),
            dma((4, 2, 2)),
            dma((4, 2, 2)),
            dma((2,)),
            dma((2,)),
            dma((2, 8)),
            dma((2, 8)),
            dma((2, 3)),
            dma((2, 3)),
            dma((2 * n - 1,)),
            dma((2 * n - 1,)),
        ],
        compiler_params=pltpu.CompilerParams(
            collective_id=0, has_side_effects=True, vmem_limit_bytes=56 * 2**20
        ),
        cost_estimate=pl.CostEstimate(flops=6 * 10**9, bytes_accessed=12 * 2**20, transcendentals=0),
    )(receptor[0], channel_weight, owners, rotations, own, forward, inverse, lines, back_lines, mirror, fold)
    scores, best, best_all = pl.pallas_call(
        write_kernel,
        out_shape=(
            jax.ShapeDtypeStruct((2, 2, G, CELLS), BF16),
            jax.ShapeDtypeStruct((1, 1, 2, 2), F32),
            jax.ShapeDtypeStruct((1, 2, 2), F32),
        ),
        in_specs=[hbm, hbm],
        out_specs=(hbm, hbm, hbm),
        scratch_shapes=[
            pltpu.VMEM((2, 2, G, CELLS), BF16),
            pltpu.VMEM((2, 8, LANES), F32),
            pltpu.VMEM((1, 1, 2, 2), F32),
            pltpu.VMEM((1, 2, 2), F32),
            dma((3,)),
            dma((4,)),
        ],
        cost_estimate=pl.CostEstimate(flops=0, bytes_accessed=2**19, transcendentals=0),
    )(scores, tops)
    return scores[None, None], best, best_all


def solution(mesh):
    in_specs = (
        P("rec", None, "lig", None),
        P("lig", "rec", None, None, None, None),
        P(),
        P("lig", None),
        P("lig", None, None),
    )
    out_specs = (
        P("rec", "lig", None, None, None, None),
        P("rec", "lig", None, None),
        P("lig", None, None),
    )
    body = functools.partial(on_device, n=mesh.shape["rec"] // 2, ligs=mesh.shape["lig"])
    return jax.shard_map(body, mesh=mesh, in_specs=in_specs, out_specs=out_specs, check_vma=False)
```
